128 devices in a mesh: ctx: 16 (over x, y_hi, core), head: 8 (over y_lo, z).
Axes of the slice: x: 4, y: 4 (y_hi: 2, y_lo: 2; y = y_hi * 2 + y_lo), z: 4, core: 2. Of those that a mesh axis runs over, the one named last changes fastest.
Arguments:
- queries: bfloat16 [8192, 8192], P('ctx', 'head'), may hold values from -100 to 100
- key_states: bfloat16 [8192, 1024], P('ctx', 'head'), may hold values from -4.5 to 4.5
- value_states: bfloat16 [8192, 1024], P('ctx', 'head'), may hold values from -6 to 6
- doc_ids: int32 [8192], P('ctx'), may hold values from 0 to 7, never falling along the last dimension, each value on 1 to 4096 neighbouring positions
- out_weight: bfloat16 [8192, 4096], P('head'), may hold values from -0.0625 to 0.0625
Outputs:
- projected: bfloat16 [8192, 4096], P(('ctx', 'head'))
The draws below stay inside these ranges and needn't reach their ends.
Inputs may be any that keep to these rules, and one draw needn't show every extreme that they name: `doc_ids`: never falling along the sequence; each document has 1 to 4096 tokens, one exactly 4096.
All inputs are finite; a program needn't handle non-finite values.
Results may differ from the reference program's by a relative error of at most 0.018.
Values may be sent and summed in bfloat16 or wider, within the bound.
A program may use at most 64 MiB of HBM per device.

```python
import math
import jax
import jax.numpy as jnp
import numpy as np
from jax import lax

DH = 128
Q_PER_KV = 8
D_OUT = 4096
DOCS = 8
KV_HEADS = 8
HEADS = 64
TOKENS = 8192
DOC_MOST = 4096
N_HEAD = 8


def shared_keys(key):
    return jnp.clip(jax.random.normal(key, (TOKENS, KV_HEADS * DH), jnp.float32), -4.5, 4.5)


def draw_key_states(key, part):
    key_base = shared_keys(key)
    return key_base.astype(jnp.bfloat16)


def draw_queries(key, part):
    key = jax.random.fold_in(key, 12)
    fresh = jnp.clip(jax.random.normal(key, (TOKENS, HEADS * DH), jnp.float32), -4.5, 4.5)
    return fresh.astype(jnp.bfloat16)


def level_of(rng, shape, pieces, low, top_value):
    def one(position, shards_of):
        draws = jax.random.uniform(jax.random.fold_in(jax.random.fold_in(rng, 6), position), (shards_of,), jnp.float32, low / len(pieces), top_value / len(pieces))
        return jnp.repeat(jnp.exp(draws), shape[position] // shards_of).reshape((-1,) + (1,) * (len(shape) - position - 1))

    gain = one(*pieces[0])
    for cut in pieces[1:]:
        gain = gain * one(*cut)
    return gain


def profile(amount, total, most, slope):
    portions = [(1 << 20) // math.isqrt(rank ** slope) + 1 for rank in range(2, amount + 1)]
    spare, counts = total - most - (amount - 1), [1] * (amount - 1)
    while spare > 0:
        free = [i for i in range(amount - 1) if counts[i] < most]
        whole, remaining = sum([portions[i] for i in free]), spare
        for i in free:
            addition = min(most - counts[i], max(1, remaining * portions[i] // whole), spare)
            counts[i] = counts[i] + addition
            spare = spare - addition
    return np.array([most] + counts)


def uneven_parts(stream_key, number_of, total, most, lean):
    if number_of == 2:
        one = jax.random.randint(stream_key, (), max(1, total - most), min(most, total - 1) + 1)
        return jnp.stack([one, total - one])
    sizes = jnp.asarray(profile(number_of, total, most, lean), jnp.int32)
    pairs = (number_of - 1) // 2
    giver, receiver = sizes[1:1 + 2 * pairs:2], sizes[2:2 + 2 * pairs:2]
    slack = jnp.minimum(giver - 1, most - receiver)
    moved = jax.random.randint(jax.random.fold_in(stream_key, 1), (pairs,), 0, 1 << 20) % (slack + 1)
    sizes = sizes.at[1:1 + 2 * pairs:2].set(giver - moved).at[2:2 + 2 * pairs:2].set(receiver + moved)
    return sizes[jax.random.permutation(jax.random.fold_in(stream_key, 2), number_of)]


def gaussian(rng, shape, scale, reach, shards=(), held_as=jnp.bfloat16):
    drawn = jax.random.normal(rng, shape, jnp.float32) * scale
    if len(shards) > 0:
        drawn = level_of(rng, shape, shards, -0.22, 0.18) * drawn
    return jnp.clip(drawn, min=-reach, max=reach).astype(held_as)


def setup_inputs(seed: int = 0) -> dict:
    splits = jax.random.split(jax.random.key(seed), 6)
    return {
        "queries": draw_queries(jax.random.fold_in(splits[5], 71), 0),
        "key_states": draw_key_states(jax.random.fold_in(splits[5], 71), 0),
        "value_states": gaussian(splits[2], (TOKENS, KV_HEADS * DH), 1.0, 6.0, ((0, 16), (1, 8))),
        "doc_ids": jnp.searchsorted(jnp.cumsum(uneven_parts(splits[3], DOCS, TOKENS, DOC_MOST, 1)), jnp.arange(TOKENS), side="right").astype(jnp.int32),
        "out_weight": gaussian(splits[4], (HEADS * DH, D_OUT), (HEADS * DH) ** -0.5, 0.0625, ((0, 8),)),
    }


def attend_group(group_q, group_k, group_v, doc_ids):
    q_block = math.gcd(TOKENS, 512)
    attn_scale = DH ** -0.5
    positions = jnp.arange(TOKENS, dtype=jnp.int32)
    key_f = group_k.astype(jnp.float32)
    value_f = group_v.astype(jnp.float32)

    def one_block(block_index):
        row_start = (block_index * q_block).astype(jnp.int32)
        query_blk = lax.dynamic_slice_in_dim(group_q, row_start, q_block, 0).astype(jnp.float32)
        query_pos = lax.dynamic_slice_in_dim(positions, row_start, q_block, 0)
        query_doc = lax.dynamic_slice_in_dim(doc_ids, row_start, q_block, 0)
        scores = jnp.einsum('qhd,kd->hqk', query_blk, key_f) * attn_scale
        allowed = (positions[None, :] <= query_pos[:, None]) & (doc_ids[None, :] == query_doc[:, None])
        masked = jnp.where(allowed[None], scores, -1e30)
        top_score = jnp.max(masked, axis=-1, keepdims=True)
        prob_rows = jnp.where(allowed[None], jnp.exp(masked - top_score), 0.0)
        denom_sum = jnp.sum(prob_rows, axis=-1)
        rounded = lax.optimization_barrier(prob_rows.astype(jnp.bfloat16)).astype(jnp.float32)
        weighted = jnp.einsum('hqk,kd->qhd', rounded, value_f)
        return weighted / jnp.transpose(denom_sum)[:, :, None]

    blocks = lax.map(one_block, jnp.arange(TOKENS // q_block, dtype=jnp.int32))
    return blocks.reshape(TOKENS, Q_PER_KV, DH)


def reference(queries, key_states, value_states, doc_ids, out_weight):
    grouped_q = jnp.transpose(queries.reshape(TOKENS, KV_HEADS, Q_PER_KV, DH), (1, 0, 2, 3))
    grouped_k = jnp.transpose(key_states.reshape(TOKENS, KV_HEADS, DH), (1, 0, 2))
    grouped_v = jnp.transpose(value_states.reshape(TOKENS, KV_HEADS, DH), (1, 0, 2))

    def per_head(head_index):
        return attend_group(grouped_q[head_index], grouped_k[head_index], grouped_v[head_index], doc_ids)

    attended = lax.map(per_head, jnp.arange(KV_HEADS, dtype=jnp.int32))
    attended = jnp.transpose(attended, (1, 0, 2, 3)).reshape(TOKENS, HEADS * DH).astype(jnp.bfloat16)
    group_width = HEADS * DH // N_HEAD
    attn_groups = jnp.transpose(attended.reshape(TOKENS, N_HEAD, group_width), (1, 0, 2))
    weight_groups = out_weight.reshape(N_HEAD, group_width, D_OUT)

    def add_group(running, paired):
        partial_term = jnp.dot(paired[0], paired[1], preferred_element_type=jnp.float32)
        rounded = lax.optimization_barrier(partial_term.astype(jnp.bfloat16))
        return running + rounded.astype(jnp.float32), None

    summed, unused = lax.scan(add_group, jnp.zeros((TOKENS, D_OUT), jnp.float32), (attn_groups, weight_groups))
    return summed.astype(jnp.bfloat16)
```

```python
import jax
import jax.numpy as jnp
from jax import lax
from jax.experimental import pallas as pl
from jax.experimental.pallas import tpu as pltpu
from jax.sharding import PartitionSpec as P

DH = 128
TOK = 512
VROWS = 144
BLOCK = TOK + 4 * VROWS
SLOTS = 9
UNITS = 16
D_OUT = 4096
PIECES = 4
PCOLS = D_OUT // PIECES
EXP_SCALE = DH**-0.5 * 1.4426950408889634
FAR = -1e30
MESH = pl.DeviceIdType.MESH
NT = (((1,), (1,)), ((), ()))
bf16 = jnp.bfloat16
f32 = jnp.float32


def kernel(
    q_ref, k_ref, v_ref, ids_ref, w_hbm, out_ref,
    kv, kf, qx, s0, s1, mx0, mx1, top, acc, att, w, part, own,
    r_a, r_b, r_up, r_down, y_out, y_in,
    kv_send, kv_recv, rs_send, rs_recv, w_sem,
):
    c = lax.axis_index("ctx")
    h = lax.axis_index("head")
    x = c // 4
    y_hi = (c // 2) % 2
    core = c % 2
    y_lo = h // 4
    z = h % 4

    def at_x(step):
        return (((x + step) % 4) * 4 + y_hi * 2 + core, h)

    def at_z(step):
        return (c, y_lo * 4 + (z + step) % 4)

    x_next, x_prev, x_far = at_x(1), at_x(3), at_x(2)
    y_pair = (x * 4 + (1 - y_hi) * 2 + core, h)
    sibling = (x * 4 + y_hi * 2 + 1 - core, h)
    z_next, z_prev = at_z(1), at_z(3)
    y_mate = (c, (1 - y_lo) * 4 + z)

    barrier = pltpu.get_barrier_semaphore()
    for peer in (x_next, x_prev, x_far, y_pair, sibling, z_next, z_prev, y_mate):
        pl.semaphore_signal(barrier, inc=1, device_id=peer, device_id_type=MESH)

    w_copy = pltpu.make_async_copy(w_hbm, w, w_sem)
    w_copy.start()

    kv[0, 0:TOK, :] = k_ref[...]
    sub16 = lax.broadcasted_iota(jnp.int32, (16, 128), 0)
    for r in range(4):
        base = TOK + r * VROWS
        kv[0, base : base + 128, :] = (
            v_ref[r * 128 : (r + 1) * 128, :].astype(f32).T.astype(bf16)
        )
        id_row = jnp.broadcast_to(ids_ref[r : r + 1, :].astype(f32), (16, 128))
        kv[0, base + 128 : base + VROWS, :] = jnp.where(
            sub16 == 0, 1.0, jnp.where(sub16 == 1, id_row, 0.0)
        ).astype(bf16)

    pl.semaphore_wait(barrier, 8)

    def kv_copy(src, dst, send, peer):
        return pltpu.make_async_remote_copy(
            src_ref=kv.at[src],
            dst_ref=kv.at[dst],
            send_sem=kv_send.at[send],
            recv_sem=kv_recv.at[dst],
            device_id=peer,
            device_id_type=MESH,
        )

    def arrived(slot):
        kv_copy(slot, slot, 0, sibling).wait_recv()

    kv_copy(0, 4, 0, x_next).start()

    @pl.when(y_hi == 0)
    def _():
        kv_copy(0, 2, 2, y_pair).start()

    @pl.when(core == 0)
    def _():
        kv_copy(0, 1, 4, sibling).start()

    lane = lax.broadcasted_iota(jnp.int32, (128, 128), 1).astype(f32)

    def id_columns(slot, r):
        base = TOK + r * VROWS + 128
        row = kv[slot, base : base + 16, :].astype(f32)[1:2, :]
        return jnp.broadcast_to(row, (128, 128)).T

    def key_marks(slot):
        shift = jnp.where(c >= slot, 0.0, 1000.0)
        for r in range(4):
            kf[slot, r * 128 : (r + 1) * 128, :] = jnp.where(
                id_columns(slot, r) + shift == lane, 0.0, FAR
            ).astype(bf16)

    order = (2, 1, 3, 0)
    firsts = [((z + step) % 4) * 64 for step in order]

    for r in range(4):
        kf[0, r * 128 : (r + 1) * 128, :] = jnp.where(id_columns(0, r) == lane, 1.0, 0.0).astype(bf16)
    for t in range(4):
        lo = pl.ds(pl.multiple_of(firsts[t], 64), 64)
        hi = pl.ds(pl.multiple_of(firsts[t] + 256, 64), 64)
        for half, rows in enumerate((lo, hi)):
            marks = kf[0, rows, :]
            for g in range(4):
                for j in range(2):
                    place = j * 128 + half * 64
                    head = 2 * g + j
                    qx[t * 4 + g, place : place + 64, 0:128] = q_ref[rows, head * 128 : (head + 1) * 128]
                    qx[t * 4 + g, place : place + 64, 128:256] = marks
    key_marks(0)

    key_index = lax.broadcasted_iota(jnp.int32, (TOK, 256), 0)
    lane_q = lax.broadcasted_iota(jnp.int32, (1, 256), 1) % 128

    def score(unit, slot, s_ref, mx_ref, diagonal):
        keys = jnp.concatenate([kv[slot, 0:TOK, :], kf[slot]], axis=1)
        s = lax.dot_general(keys, qx[unit], NT, preferred_element_type=f32)
        if diagonal:
            t = unit // 4
            step = jnp.where(t == 0, 2, jnp.where(t == 1, 1, jnp.where(t == 2, 3, 0)))
            first = ((z + step) % 4) * 64
            q_index = first + jnp.where(lane_q < 64, lane_q, lane_q + 192)
            s = jnp.where(key_index <= q_index, s, FAR)
        s_ref[...] = s
        mx_ref[...] = jnp.max(s, axis=0, keepdims=True)

    def gather_values(unit, slot, s_ref, mx_ref, diagonal):
        values = jnp.concatenate(
            [kv[slot, TOK + r * VROWS : TOK + (r + 1) * VROWS, :] for r in range(4)], axis=1
        )
        if diagonal:
            new_top = mx_ref[...]
        else:
            old_top = top[unit]
            new_top = jnp.maximum(old_top, mx_ref[...])
        probs = jnp.exp2((s_ref[...] - new_top) * EXP_SCALE).astype(bf16)
        add = jnp.dot(values, probs, preferred_element_type=f32)
        if diagonal:
            acc[unit] = add
        else:
            acc[unit] = acc[unit] * jnp.exp2((old_top - new_top) * EXP_SCALE) + add
        top[unit] = new_top

    def run(count, unit_of, slot_of, diagonal=False):
        score(unit_of(0), slot_of(0), s0, mx0, diagonal)

        def body(i, carry):
            a, b, n = 2 * i, 2 * i + 1, jnp.minimum(2 * i + 2, count - 1)
            score(unit_of(b), slot_of(b), s1, mx1, diagonal)
            gather_values(unit_of(a), slot_of(a), s0, mx0, diagonal)
            score(unit_of(n), slot_of(n), s0, mx0, diagonal)
            gather_values(unit_of(b), slot_of(b), s1, mx1, diagonal)
            return carry

        lax.fori_loop(0, count // 2, body, 0)

    def one_pass(slot, diagonal=False):
        run(UNITS, lambda i: i, lambda i: slot, diagonal)

    one_pass(0, True)

    arrived(4)
    kv_copy(0, 8, 1, x_far).start()

    @pl.when(y_hi == 0)
    def _():
        kv_copy(4, 6, 3, y_pair).start()

    @pl.when(y_hi == 1)
    def _():
        kv_copy(4, 2, 2, y_pair).start()

    @pl.when(core == 0)
    def _():
        kv_copy(4, 5, 6, sibling).start()

    @pl.when(core == 1)
    def _():
        kv_copy(4, 3, 5, sibling).start()

    key_marks(4)
    one_pass(4)

    arrived(2)

    @pl.when(core == 0)
    def _():
        kv_copy(2, 3, 5, sibling).start()

    @pl.when(core == 1)
    def _():
        kv_copy(2, 1, 4, sibling).start()

    key_marks(2)
    one_pass(2)

    arrived(8)

    @pl.when(y_hi == 1)
    def _():
        kv_copy(8, 6, 3, y_pair).start()

    @pl.when(core == 1)
    def _():
        kv_copy(8, 7, 7, sibling).start()

    key_marks(8)
    one_pass(8)

    arrived(6)

    @pl.when(core == 0)
    def _():
        kv_copy(6, 7, 7, sibling).start()

    @pl.when(core == 1)
    def _():
        kv_copy(6, 5, 6, sibling).start()

    key_marks(6)
    one_pass(6)

    for slot in (1, 3, 5, 7):
        arrived(slot)
        key_marks(slot)

    w_copy.wait()

    def rs_copy(kind, n):
        src, dst, peer = (
            (part.at[0, n, pl.ds(0, 64)], r_a.at[n], z_next),
            (part.at[0, n, pl.ds(64, 64)], r_b.at[n], z_prev),
            (part.at[1, n, pl.ds(64, 64)], r_up.at[n, pl.ds(64, 64)], z_next),
            (part.at[1, n, pl.ds(0, 64)], r_up.at[n, pl.ds(0, 64)], z_next),
            (part.at[2, n, pl.ds(0, 64)], r_down.at[n, pl.ds(0, 64)], z_prev),
            (part.at[2, n, pl.ds(64, 64)], r_down.at[n, pl.ds(64, 64)], z_prev),
            (y_out.at[n], y_in.at[n], y_mate),
        )[kind]
        return pltpu.make_async_remote_copy(
            src_ref=src,
            dst_ref=dst,
            send_sem=rs_send.at[kind, n],
            recv_sem=rs_recv.at[kind, n],
            device_id=peer,
            device_id_type=MESH,
        )

    for t in range(4):
        run(16, lambda i: t * 4 + i // 4, lambda i: 2 * (i % 4) + 1)
        for g in range(4):
            state = acc[t * 4 + g]
            rows = state[0:128] / state[128:129]
            for j in range(2):
                head = 2 * g + j
                att[:, head * 128 : (head + 1) * 128] = rows[:, j * 128 : (j + 1) * 128].T.astype(bf16)

        def project(n, carry):
            cols = pl.ds(pl.multiple_of(n * PCOLS, PCOLS), PCOLS)
            piece = jnp.dot(att[...], w[:, cols], preferred_element_type=f32).astype(bf16)
            if t < 3:
                part[t, n] = piece
            else:
                own[n] = piece
            if t == 0:
                rs_copy(0, n).start()
                rs_copy(1, n).start()
            if t == 1:
                rs_copy(2, n).start()
            if t == 2:
                rs_copy(4, n).start()
            return carry

        lax.fori_loop(0, PIECES, project, 0)

    def pass_on(n, carry):
        rs_copy(0, n).wait_recv()
        part[1, n, 0:64] = (part[1, n, 0:64].astype(f32) + r_a[n].astype(f32)).astype(bf16)
        rs_copy(3, n).start()
        rs_copy(1, n).wait_recv()
        part[2, n, 64:128] = (part[2, n, 64:128].astype(f32) + r_b[n].astype(f32)).astype(bf16)
        rs_copy(5, n).start()
        return carry

    lax.fori_loop(0, PIECES, pass_on, 0)

    def total(n, first):
        rows = pl.ds(pl.multiple_of(first, 64), 64)
        return own[n, rows].astype(f32) + r_up[n, rows].astype(f32) + r_down[n, rows].astype(f32)

    def collect(n, carry):
        for kind in (2, 3, 4, 5):
            rs_copy(kind, n).wait_recv()
        y_out[n] = total(n, 64 - y_lo * 64).astype(bf16)
        rs_copy(6, n).start()
        return carry

    lax.fori_loop(0, PIECES, collect, 0)

    for n in range(PIECES):
        rs_copy(6, n).wait_recv()
        out_ref[:, n * PCOLS : (n + 1) * PCOLS] = (total(n, y_lo * 64) + y_in[n].astype(f32)).astype(bf16)

    for send in range(8):
        kv_copy(0, 0, send, sibling).wait_send()

    def sent(n, carry):
        for kind in range(7):
            rs_copy(kind, n).wait_send()
        return carry

    lax.fori_loop(0, PIECES, sent, 0)


def on_device(queries, key_states, value_states, doc_ids, out_weight):
    vmem = pl.BlockSpec(memory_space=pltpu.VMEM)
    return pl.pallas_call(
        kernel,
        name="attend_project",
        out_shape=jax.ShapeDtypeStruct((64, D_OUT), bf16),
        in_specs=[vmem, vmem, vmem, vmem, pl.BlockSpec(memory_space=pl.ANY)],
        out_specs=vmem,
        scratch_shapes=[
            pltpu.VMEM((SLOTS, BLOCK, 128), bf16),
            pltpu.VMEM((SLOTS, TOK, 128), bf16),
            pltpu.VMEM((UNITS, 256, 256), bf16),
            pltpu.VMEM((TOK, 256), f32),
            pltpu.VMEM((TOK, 256), f32),
            pltpu.VMEM((1, 256), f32),
            pltpu.VMEM((1, 256), f32),
            pltpu.VMEM((UNITS, 1, 256), f32),
            pltpu.VMEM((UNITS, VROWS, 256), f32),
            pltpu.VMEM((128, 1024), bf16),
            pltpu.VMEM((1024, D_OUT), bf16),
            pltpu.VMEM((3, PIECES, 128, PCOLS), bf16),
            pltpu.VMEM((PIECES, 128, PCOLS), bf16),
            pltpu.VMEM((PIECES, 64, PCOLS), bf16),
            pltpu.VMEM((PIECES, 64, PCOLS), bf16),
            pltpu.VMEM((PIECES, 128, PCOLS), bf16),
            pltpu.VMEM((PIECES, 128, PCOLS), bf16),
            pltpu.VMEM((PIECES, 64, PCOLS), bf16),
            pltpu.VMEM((PIECES, 64, PCOLS), bf16),
            pltpu.SemaphoreType.DMA((8,)),
            pltpu.SemaphoreType.DMA((SLOTS,)),
            pltpu.SemaphoreType.DMA((7, PIECES)),
            pltpu.SemaphoreType.DMA((7, PIECES)),
            pltpu.SemaphoreType.DMA,
        ],
        compiler_params=pltpu.CompilerParams(
            collective_id=0, has_side_effects=True, vmem_limit_bytes=56 * 2**20
        ),
        cost_estimate=pl.CostEstimate(
            flops=14 * 10**9, bytes_accessed=10 * 2**20, transcendentals=19 * 10**6
        ),
    )(queries, key_states, value_states, doc_ids.reshape(4, 128), out_weight)


def solution(mesh):
    return jax.shard_map(
        on_device,
        mesh=mesh,
        in_specs=(P("ctx", "head"), P("ctx", "head"), P("ctx", "head"), P("ctx"), P("head", None)),
        out_specs=P(("ctx", "head"), None),
        check_vma=False,
    )
```

```python
import jax
import jax.numpy as jnp
from jax import lax
from jax.experimental import pallas as pl
from jax.experimental.pallas import tpu as pltpu
from jax.sharding import PartitionSpec as P

DH = 128
TOK = 512
VROWS = 144
BLOCK = TOK + 4 * VROWS
SLOTS = 9
UNITS = 16
D_OUT = 4096
PCOLS = 512
NY, NZ = 3, 5
EXP_SCALE = DH**-0.5 * 1.4426950408889634
FAR = -1e30
MESH = pl.DeviceIdType.MESH
NT = (((1,), (1,)), ((), ()))
bf16 = jnp.bfloat16
f32 = jnp.float32


def kernel(
    q_ref, k_ref, v_ref, ids_ref, w_hbm, out_ref,
    kv, kf, qx, s0, s1, mx0, mx1, top, acc, att, w,
    part_z, a_z, b_z, up_z, down_z, mate_out, mate_in,
    part_y, met_y, sum_y, a_y, b_y, up_y, down_y,
    kv_send, kv_recv, z_send, z_recv, y_send, y_recv, w_sem,
):
    c = lax.axis_index("ctx")
    h = lax.axis_index("head")
    x = c // 4
    y_hi = (c // 2) % 2
    core = c % 2
    y_lo = h // 4
    z = h % 4

    def at_x(step):
        return (((x + step) % 4) * 4 + y_hi * 2 + core, h)

    def at_z(step):
        return (c, y_lo * 4 + (z + step) % 4)

    x_next, x_prev, x_far = at_x(1), at_x(3), at_x(2)
    y_pair = (x * 4 + (1 - y_hi) * 2 + core, h)
    sibling = (x * 4 + y_hi * 2 + 1 - core, h)
    z_next, z_prev = at_z(1), at_z(3)
    y_mate = (c, (1 - y_lo) * 4 + z)

    barrier = pltpu.get_barrier_semaphore()
    for peer in (x_next, x_prev, x_far, y_pair, sibling, z_next, z_prev, y_mate):
        pl.semaphore_signal(barrier, inc=1, device_id=peer, device_id_type=MESH)

    w_copy = pltpu.make_async_copy(w_hbm, w, w_sem)
    w_copy.start()

    kv[0, 0:TOK, :] = k_ref[...]
    sub16 = lax.broadcasted_iota(jnp.int32, (16, 128), 0)
    for r in range(4):
        base = TOK + r * VROWS
        kv[0, base : base + 128, :] = (
            v_ref[r * 128 : (r + 1) * 128, :].astype(f32).T.astype(bf16)
        )
        id_row = jnp.broadcast_to(ids_ref[r : r + 1, :].astype(f32), (16, 128))
        kv[0, base + 128 : base + VROWS, :] = jnp.where(
            sub16 == 0, 1.0, jnp.where(sub16 == 1, id_row, 0.0)
        ).astype(bf16)

    pl.semaphore_wait(barrier, 8)

    def kv_copy(src, dst, send, peer):
        return pltpu.make_async_remote_copy(
            src_ref=kv.at[src],
            dst_ref=kv.at[dst],
            send_sem=kv_send.at[send],
            recv_sem=kv_recv.at[dst],
            device_id=peer,
            device_id_type=MESH,
        )

    def arrived(slot):
        kv_copy(slot, slot, 0, sibling).wait_recv()

    kv_copy(0, 4, 0, x_next).start()

    @pl.when(y_hi == 0)
    def _():
        kv_copy(0, 2, 2, y_pair).start()

    @pl.when(core == 0)
    def _():
        kv_copy(0, 1, 4, sibling).start()

    lane = lax.broadcasted_iota(jnp.int32, (128, 128), 1).astype(f32)

    def id_columns(slot, r):
        base = TOK + r * VROWS + 128
        row = kv[slot, base : base + 16, :].astype(f32)[1:2, :]
        return jnp.broadcast_to(row, (128, 128)).T

    def key_marks(slot):
        shift = jnp.where(c >= slot, 0.0, 1000.0)
        for r in range(4):
            kf[slot, r * 128 : (r + 1) * 128, :] = jnp.where(
                id_columns(slot, r) + shift == lane, 0.0, FAR
            ).astype(bf16)

    order = (2, 1, 3, 0)
    firsts = [((z + step) % 4) * 64 for step in order]

    for r in range(4):
        kf[0, r * 128 : (r + 1) * 128, :] = jnp.where(id_columns(0, r) == lane, 1.0, 0.0).astype(bf16)
    for t in range(4):
        lo = pl.ds(pl.multiple_of(firsts[t], 64), 64)
        hi = pl.ds(pl.multiple_of(firsts[t] + 256, 64), 64)
        for half, rows in enumerate((lo, hi)):
            marks = kf[0, rows, :]
            for g in range(4):
                for j in range(2):
                    place = j * 128 + half * 64
                    head = 2 * g + j
                    qx[t * 4 + g, place : place + 64, 0:128] = q_ref[rows, head * 128 : (head + 1) * 128]
                    qx[t * 4 + g, place : place + 64, 128:256] = marks
    key_marks(0)

    key_index = lax.broadcasted_iota(jnp.int32, (TOK, 256), 0)
    lane_q = lax.broadcasted_iota(jnp.int32, (1, 256), 1) % 128

    def score(unit, slot, i, s_ref, diagonal):
        keys = jnp.concatenate([kv[slot, 0:TOK, :], kf[slot]], axis=1)
        s = lax.dot_general(keys, qx[unit], NT, preferred_element_type=f32)
        if diagonal:
            t = unit // 4
            step = jnp.where(t == 0, 2, jnp.where(t == 1, 1, jnp.where(t == 2, 3, 0)))
            first = ((z + step) % 4) * 64
            q_index = first + jnp.where(lane_q < 64, lane_q, lane_q + 192)
            s = jnp.where(key_index <= q_index, s, FAR)
        s_ref[i * TOK : (i + 1) * TOK, :] = s
        return jnp.max(s.reshape(TOK // 8, 8, 256), axis=0)

    def weigh(slot, i, s_ref, new_top):
        values = jnp.concatenate(
            [kv[slot, TOK + r * VROWS : TOK + (r + 1) * VROWS, :] for r in range(4)], axis=1
        )
        probs = jnp.exp2((s_ref[i * TOK : (i + 1) * TOK, :] - new_top) * EXP_SCALE).astype(bf16)
        return jnp.dot(values, probs, preferred_element_type=f32)

    def stage(ahead, now, slots, into, held, diagonal):
        if now is not None:
            new_top = jnp.max(held[1][...], axis=0, keepdims=True)
            if not diagonal:
                old_top = top[now]
                new_top = jnp.maximum(old_top, new_top)
        highest, add = None, None
        for i, slot in enumerate(slots):
            if ahead is not None:
                here = score(ahead, slot, i, into[0], diagonal)
                highest = here if highest is None else jnp.maximum(highest, here)
            if now is not None:
                here = weigh(slot, i, held[0], new_top)
                add = here if add is None else add + here
        if ahead is not None:
            into[1][...] = highest
        if now is not None:
            if diagonal:
                acc[now] = add
            else:
                acc[now] = acc[now] * jnp.exp2((old_top - new_top) * EXP_SCALE) + add
            top[now] = new_top

    pair = ((s0, mx0), (s1, mx1))

    def run(first, count, slots, diagonal=False):
        stage(first, None, slots, pair[0], None, diagonal)

        def body(i, carry):
            for e in range(4):
                now = first + 4 * i + e
                ahead = now + 1
                if e == 3:
                    ahead = None if count == 4 else jnp.minimum(ahead, first + count - 1)
                stage(ahead, now, slots, pair[(e + 1) % 2], pair[e % 2], diagonal)
            return carry

        if count == 4:
            body(0, 0)
        else:
            lax.fori_loop(0, count // 4, body, 0)

    run(0, UNITS, (0,), True)

    arrived(4)
    kv_copy(0, 8, 1, x_far).start()

    @pl.when(y_hi == 0)
    def _():
        kv_copy(4, 6, 3, y_pair).start()

    @pl.when(y_hi == 1)
    def _():
        kv_copy(4, 2, 2, y_pair).start()

    @pl.when(core == 0)
    def _():
        kv_copy(4, 5, 6, sibling).start()

    @pl.when(core == 1)
    def _():
        kv_copy(4, 3, 5, sibling).start()

    key_marks(4)
    run(0, UNITS, (4,))

    arrived(2)

    @pl.when(core == 0)
    def _():
        kv_copy(2, 3, 5, sibling).start()

    @pl.when(core == 1)
    def _():
        kv_copy(2, 1, 4, sibling).start()

    key_marks(2)

    arrived(8)

    @pl.when(y_hi == 1)
    def _():
        kv_copy(8, 6, 3, y_pair).start()

    @pl.when(core == 1)
    def _():
        kv_copy(8, 7, 7, sibling).start()

    key_marks(8)
    run(0, UNITS, (2, 8))

    for slot in (1, 3):
        arrived(slot)
        key_marks(slot)

    arrived(6)

    @pl.when(core == 0)
    def _():
        kv_copy(6, 7, 7, sibling).start()

    @pl.when(core == 1)
    def _():
        kv_copy(6, 5, 6, sibling).start()

    key_marks(6)

    for slot in (5, 7):
        arrived(slot)
        key_marks(slot)

    w_copy.wait()

    def z_copy(kind, n):
        low, high = pl.ds(0, 64), pl.ds(64, 64)
        src, dst, peer = (
            (part_z.at[0, n, low], a_z.at[n], z_next),
            (part_z.at[0, n, high], b_z.at[n], z_prev),
            (part_z.at[1, n, high], up_z.at[n, high], z_next),
            (part_z.at[1, n, low], up_z.at[n, low], z_next),
            (part_z.at[2, n, low], down_z.at[n, low], z_prev),
            (part_z.at[2, n, high], down_z.at[n, high], z_prev),
            (mate_out.at[n], mate_in.at[n], y_mate),
        )[kind]
        return pltpu.make_async_remote_copy(
            src_ref=src, dst_ref=dst, send_sem=z_send.at[kind, n], recv_sem=z_recv.at[kind, n],
            device_id=peer, device_id_type=MESH,
        )

    mine = pl.ds(pl.multiple_of(y_lo * 64, 64), 64)
    theirs = pl.ds(pl.multiple_of(64 - y_lo * 64, 64), 64)

    def y_copy(kind, n):
        low, high = pl.ds(0, 32), pl.ds(32, 32)
        if kind < 4:
            src, dst, peer = part_y.at[kind, n, theirs], met_y.at[kind, n], y_mate
        else:
            src, dst, peer = (
                (sum_y.at[0, n, low], a_y.at[n], z_next),
                (sum_y.at[0, n, high], b_y.at[n], z_prev),
                (sum_y.at[1, n, high], up_y.at[n, high], z_next),
                (sum_y.at[1, n, low], up_y.at[n, low], z_next),
                (sum_y.at[2, n, low], down_y.at[n, low], z_prev),
                (sum_y.at[2, n, high], down_y.at[n, high], z_prev),
            )[kind - 4]
        return pltpu.make_async_remote_copy(
            src_ref=src, dst_ref=dst, send_sem=y_send.at[kind, n], recv_sem=y_recv.at[kind, n],
            device_id=peer, device_id_type=MESH,
        )

    def meet(t):
        for n in range(NY):
            y_copy(t, n).wait_recv()
            sum_y[t, n] = (part_y[t, n, mine].astype(f32) + met_y[t, n].astype(f32)).astype(bf16)
            for kind in ((4, 5), (6,), (8,))[t]:
                y_copy(kind, n).start()

    def add_far_z(t):
        for n in range(NZ):
            z_copy(t - 1, n).wait_recv()
            if t == 1:
                part_z[1, n, 0:64] = (part_z[1, n, 0:64].astype(f32) + a_z[n].astype(f32)).astype(bf16)
                z_copy(3, n).start()
            else:
                part_z[2, n, 64:128] = (part_z[2, n, 64:128].astype(f32) + b_z[n].astype(f32)).astype(bf16)
                z_copy(5, n).start()

    def add_far_y(t):
        for n in range(NY):
            y_copy(3 + t, n).wait_recv()
            if t == 1:
                sum_y[1, n, 0:32] = (sum_y[1, n, 0:32].astype(f32) + a_y[n].astype(f32)).astype(bf16)
                y_copy(7, n).start()
            else:
                sum_y[2, n, 32:64] = (sum_y[2, n, 32:64].astype(f32) + b_y[n].astype(f32)).astype(bf16)
                y_copy(9, n).start()

    for t in range(4):
        run(t * 4, 4, (6, 1, 3, 5, 7))
        for g in range(4):
            state = acc[t * 4 + g]
            rows = state[0:128] / state[128:129]
            for j in range(2):
                head = 2 * g + j
                att[:, head * 128 : (head + 1) * 128] = rows[:, j * 128 : (j + 1) * 128].T.astype(bf16)

        for n in range(NY + NZ):
            piece = jnp.dot(
                att[...], w[:, n * PCOLS : (n + 1) * PCOLS], preferred_element_type=f32
            ).astype(bf16)
            if n < NY:
                part_y[t, n] = piece
            else:
                part_z[t, n - NY] = piece
            if n == NY - 1:
                for i in range(NY):
                    y_copy(t, i).start()
        for n in range(NZ):
            for kind in ((0, 1), (2,), (4,), ())[t]:
                z_copy(kind, n).start()
        if t > 0:
            meet(t - 1)
        if t > 1:
            add_far_z(t - 1)

    add_far_y(1)
    add_far_y(2)

    def total_z(n, rows):
        return (
            part_z[3, n, rows].astype(f32) + up_z[n, rows].astype(f32) + down_z[n, rows].astype(f32)
        )

    for n in range(NZ):
        for kind in (2, 3, 4, 5):
            z_copy(kind, n).wait_recv()
        mate_out[n] = total_z(n, theirs).astype(bf16)
        z_copy(6, n).start()

    for n in range(NY):
        for kind in (3, 6, 7, 8, 9):
            y_copy(kind, n).wait_recv()
        out_ref[:, n * PCOLS : (n + 1) * PCOLS] = (
            part_y[3, n, mine].astype(f32) + met_y[3, n].astype(f32)
            + up_y[n].astype(f32) + down_y[n].astype(f32)
        ).astype(bf16)

    for n in range(NZ):
        z_copy(6, n).wait_recv()
        out_ref[:, (NY + n) * PCOLS : (NY + n + 1) * PCOLS] = (
            total_z(n, mine) + mate_in[n].astype(f32)
        ).astype(bf16)

    for send in range(8):
        kv_copy(0, 0, send, sibling).wait_send()
    for n in range(NZ):
        for kind in range(7):
            z_copy(kind, n).wait_send()
    for n in range(NY):
        for kind in range(10):
            y_copy(kind, n).wait_send()


def on_device(queries, key_states, value_states, doc_ids, out_weight):
    vmem = pl.BlockSpec(memory_space=pltpu.VMEM)
    return pl.pallas_call(
        kernel,
        name="attend_project",
        out_shape=jax.ShapeDtypeStruct((64, D_OUT), bf16),
        in_specs=[vmem, vmem, vmem, vmem, pl.BlockSpec(memory_space=pl.ANY)],
        out_specs=vmem,
        scratch_shapes=[
            pltpu.VMEM((SLOTS, BLOCK, 128), bf16),
            pltpu.VMEM((SLOTS, TOK, 128), bf16),
            pltpu.VMEM((UNITS, 256, 256), bf16),
            pltpu.VMEM((5 * TOK, 256), f32),
            pltpu.VMEM((5 * TOK, 256), f32),
            pltpu.VMEM((8, 256), f32),
            pltpu.VMEM((8, 256), f32),
            pltpu.VMEM((UNITS, 1, 256), f32),
            pltpu.VMEM((UNITS, VROWS, 256), f32),
            pltpu.VMEM((128, 1024), bf16),
            pltpu.VMEM((1024, D_OUT), bf16),
            pltpu.VMEM((4, NZ, 128, PCOLS), bf16),
            pltpu.VMEM((NZ, 64, PCOLS), bf16),
            pltpu.VMEM((NZ, 64, PCOLS), bf16),
            pltpu.VMEM((NZ, 128, PCOLS), bf16),
            pltpu.VMEM((NZ, 128, PCOLS), bf16),
            pltpu.VMEM((NZ, 64, PCOLS), bf16),
            pltpu.VMEM((NZ, 64, PCOLS), bf16),
            pltpu.VMEM((4, NY, 128, PCOLS), bf16),
            pltpu.VMEM((4, NY, 64, PCOLS), bf16),
            pltpu.VMEM((3, NY, 64, PCOLS), bf16),
            pltpu.VMEM((NY, 32, PCOLS), bf16),
            pltpu.VMEM((NY, 32, PCOLS), bf16),
            pltpu.VMEM((NY, 64, PCOLS), bf16),
            pltpu.VMEM((NY, 64, PCOLS), bf16),
            pltpu.SemaphoreType.DMA((8,)),
            pltpu.SemaphoreType.DMA((SLOTS,)),
            pltpu.SemaphoreType.DMA((7, NZ)),
            pltpu.SemaphoreType.DMA((7, NZ)),
            pltpu.SemaphoreType.DMA((10, NY)),
            pltpu.SemaphoreType.DMA((10, NY)),
            pltpu.SemaphoreType.DMA,
        ],
        compiler_params=pltpu.CompilerParams(
            collective_id=0, has_side_effects=True, vmem_limit_bytes=56 * 2**20
        ),
        cost_estimate=pl.CostEstimate(
            flops=14 * 10**9, bytes_accessed=10 * 2**20, transcendentals=19 * 10**6
        ),
    )(queries, key_states, value_states, doc_ids.reshape(4, 128), out_weight)


def solution(mesh):
    return jax.shard_map(
        on_device,
        mesh=mesh,
        in_specs=(P("ctx", "head"), P("ctx", "head"), P("ctx", "head"), P("ctx"), P("head", None)),
        out_specs=P(("ctx", "head"), None),
        check_vma=False,
    )
```

```python
import jax
import jax.numpy as jnp
from jax import lax
from jax.experimental import pallas as pl
from jax.experimental.pallas import tpu as pltpu
from jax.sharding import PartitionSpec as P

DH = 128
TOK = 512
VROWS = 144
BLOCK = TOK + 4 * VROWS
SLOTS = 9
RELAY_X, RELAY_Y = 9, 10
UNITS = 16
D_OUT = 4096
PCOLS = 512
NY, NZ = 3, 5
EXP_SCALE = DH**-0.5 * 1.4426950408889634
FAR = -1e30
MESH = pl.DeviceIdType.MESH
NT = (((1,), (1,)), ((), ()))
bf16 = jnp.bfloat16
f32 = jnp.float32


def kernel(
    q_hbm, k_ref, v_ref, ids_ref, w_hbm, out_ref,
    kv, kf, qx, s0, s1, mx0, mx1, top, acc, att, w,
    part_z, a_z, b_z, up_z, down_z, mate_out, mate_in,
    part_y, met_y, sum_y, a_y, b_y, up_y, down_y,
    kv_send, kv_recv, z_send, z_recv, y_send, y_recv, w_sem, q_ref, q_sem,
):
    c = lax.axis_index("ctx")
    h = lax.axis_index("head")
    x = c // 4
    y_hi = (c // 2) % 2
    core = c % 2
    y_lo = h // 4
    z = h % 4

    def at_x(step):
        return (((x + step) % 4) * 4 + y_hi * 2 + core, h)

    def at_z(step):
        return (c, y_lo * 4 + (z + step) % 4)

    x_next, x_prev, x_far = at_x(1), at_x(3), at_x(2)
    y_pair = (x * 4 + (1 - y_hi) * 2 + core, h)
    sibling = (x * 4 + y_hi * 2 + 1 - core, h)
    z_next, z_prev = at_z(1), at_z(3)
    y_mate = (c, (1 - y_lo) * 4 + z)

    barrier = pltpu.get_barrier_semaphore()
    for peer in (x_next, x_prev, x_far, y_pair, sibling, z_next, z_prev, y_mate):
        pl.semaphore_signal(barrier, inc=1, device_id=peer, device_id_type=MESH)

    q_copy = pltpu.make_async_copy(q_hbm, q_ref, q_sem)
    q_copy.start()
    w_copy = pltpu.make_async_copy(w_hbm, w, w_sem)
    w_copy.start()

    kv[0, 0:TOK, :] = k_ref[...]
    sub16 = lax.broadcasted_iota(jnp.int32, (16, 128), 0)
    for r in range(4):
        base = TOK + r * VROWS
        kv[0, base : base + 128, :] = (
            v_ref[r * 128 : (r + 1) * 128, :].astype(f32).T.astype(bf16)
        )
        id_row = jnp.broadcast_to(ids_ref[r : r + 1, :].astype(f32), (16, 128))
        kv[0, base + 128 : base + VROWS, :] = jnp.where(
            sub16 == 0, 1.0, jnp.where(sub16 == 1, id_row, 0.0)
        ).astype(bf16)

    pl.semaphore_wait(barrier, 8)

    def kv_copy(src, dst, send, peer):
        return pltpu.make_async_remote_copy(
            src_ref=kv.at[src],
            dst_ref=kv.at[dst],
            send_sem=kv_send.at[send],
            recv_sem=kv_recv.at[dst],
            device_id=peer,
            device_id_type=MESH,
        )

    def arrived(slot):
        kv_copy(slot, slot, 0, sibling).wait_recv()

    @pl.when(y_hi == 0)
    def _():
        kv_copy(0, 4, 0, x_next).start()
        kv_copy(0, 2, 1, y_pair).start()
        kv_copy(0, RELAY_X, 2, x_prev).start()

    @pl.when(y_hi == 1)
    def _():
        kv_copy(0, 8, 0, x_far).start()
        kv_copy(0, RELAY_Y, 1, y_pair).start()

    def share(slot):
        @pl.when(core == 0)
        def _():
            if slot < 8:
                kv_copy(slot, slot + 1, 6 + slot // 2, sibling).start()

        @pl.when(core == 1)
        def _():
            if slot > 0:
                kv_copy(slot, slot - 1, 5 + slot // 2, sibling).start()

    share(0)

    lane = lax.broadcasted_iota(jnp.int32, (128, 128), 1).astype(f32)

    def id_columns(slot, r):
        base = TOK + r * VROWS + 128
        row = kv[slot, base : base + 16, :].astype(f32)[1:2, :]
        return jnp.broadcast_to(row, (128, 128)).T

    def key_marks(slot):
        shift = jnp.where(c >= slot, 0.0, 1000.0)
        for r in range(4):
            kf[slot, r * 128 : (r + 1) * 128, :] = jnp.where(
                id_columns(slot, r) + shift == lane, 0.0, FAR
            ).astype(bf16)

    order = (2, 1, 3, 0)
    firsts = [((z + step) % 4) * 64 for step in order]

    q_copy.wait()

    for r in range(4):
        kf[0, r * 128 : (r + 1) * 128, :] = jnp.where(id_columns(0, r) == lane, 1.0, 0.0).astype(bf16)
    for t in range(4):
        lo = pl.ds(pl.multiple_of(firsts[t], 64), 64)
        hi = pl.ds(pl.multiple_of(firsts[t] + 256, 64), 64)
        for half, rows in enumerate((lo, hi)):
            marks = kf[0, rows, :]
            for g in range(4):
                for j in range(2):
                    place = j * 128 + half * 64
                    head = 2 * g + j
                    qx[t * 4 + g, place : place + 64, 0:128] = q_ref[rows, head * 128 : (head + 1) * 128]
                    qx[t * 4 + g, place : place + 64, 128:256] = marks
    key_marks(0)

    key_index = lax.broadcasted_iota(jnp.int32, (TOK, 256), 0)
    lane_q = lax.broadcasted_iota(jnp.int32, (1, 256), 1) % 128

    def score(unit, slot, i, s_ref, diagonal):
        keys = jnp.concatenate([kv[slot, 0:TOK, :], kf[slot]], axis=1)
        s = lax.dot_general(keys, qx[unit], NT, preferred_element_type=f32)
        if diagonal:
            t = unit // 4
            step = jnp.where(t == 0, 2, jnp.where(t == 1, 1, jnp.where(t == 2, 3, 0)))
            first = ((z + step) % 4) * 64
            q_index = first + jnp.where(lane_q < 64, lane_q, lane_q + 192)
            s = jnp.where(key_index <= q_index, s, FAR)
        s_ref[i * TOK : (i + 1) * TOK, :] = s
        return jnp.max(s.reshape(TOK // 8, 8, 256), axis=0)

    def weigh(slot, i, s_ref, new_top):
        values = jnp.concatenate(
            [kv[slot, TOK + r * VROWS : TOK + (r + 1) * VROWS, :] for r in range(4)], axis=1
        )
        probs = jnp.exp2((s_ref[i * TOK : (i + 1) * TOK, :] - new_top) * EXP_SCALE).astype(bf16)
        return jnp.dot(values, probs, preferred_element_type=f32)

    def stage(ahead, now, slots, into, held, diagonal):
        if now is not None:
            new_top = jnp.max(held[1][...], axis=0, keepdims=True)
            if not diagonal:
                old_top = top[now]
                new_top = jnp.maximum(old_top, new_top)
        highest, add = None, None
        for i, slot in enumerate(slots):
            if ahead is not None:
                here = score(ahead, slot, i, into[0], diagonal)
                highest = here if highest is None else jnp.maximum(highest, here)
            if now is not None:
                here = weigh(slot, i, held[0], new_top)
                add = here if add is None else add + here
        if ahead is not None:
            into[1][...] = highest
        if now is not None:
            if diagonal:
                acc[now] = add
            else:
                acc[now] = acc[now] * jnp.exp2((old_top - new_top) * EXP_SCALE) + add
            top[now] = new_top

    pair = ((s0, mx0), (s1, mx1))

    def run(first, count, slots, diagonal=False):
        stage(first, None, slots, pair[0], None, diagonal)

        def body(i, carry):
            for e in range(4):
                now = first + 4 * i + e
                ahead = now + 1
                if e == 3:
                    ahead = None if count == 4 else jnp.minimum(ahead, first + count - 1)
                stage(ahead, now, slots, pair[(e + 1) % 2], pair[e % 2], diagonal)
            return carry

        if count == 4:
            body(0, 0)
        else:
            lax.fori_loop(0, count // 4, body, 0)

    run(0, UNITS, (0,), True)

    @pl.when(y_hi == 0)
    def _():
        arrived(4)
        kv_copy(4, 6, 3, y_pair).start()
        share(4)
        arrived(RELAY_X)
        kv_copy(RELAY_X, 8, 4, x_prev).start()
        arrived(RELAY_Y)
        kv_copy(RELAY_Y, 2, 5, x_next).start()

    @pl.when(y_hi == 1)
    def _():
        arrived(8)
        kv_copy(8, 6, 3, y_pair).start()
        kv_copy(0, 4, 2, x_next).start()
        share(8)
        arrived(2)
        share(2)

    early = (4 + 4 * y_hi, 2 * y_hi + (1 - y_hi) * (3 + 2 * core))
    late = (
        1, 2 + y_hi, 4 * y_hi + (1 - y_hi) * (5 - 2 * core), 6 - y_hi, 7 - y_hi, 8 - y_hi,
    )
    key_marks(early[0])

    @pl.when(y_hi == 0)
    def _():
        @pl.when(core == 0)
        def _():
            arrived(3)

        @pl.when(core == 1)
        def _():
            arrived(5)

    key_marks(early[1])
    run(0, UNITS, early)

    @pl.when(y_hi == 0)
    def _():
        arrived(2)
        share(2)
        arrived(6)
        share(6)
        arrived(8)
        share(8)

        @pl.when(core == 0)
        def _():
            arrived(5)

        @pl.when(core == 1)
        def _():
            arrived(3)

    @pl.when(y_hi == 1)
    def _():
        arrived(4)
        share(4)
        arrived(6)
        share(6)
        arrived(3)
        arrived(5)

    arrived(1)
    arrived(7)
    for slot in late:
        key_marks(slot)

    w_copy.wait()

    def z_copy(kind, n):
        low, high = pl.ds(0, 64), pl.ds(64, 64)
        src, dst, peer = (
            (part_z.at[0, n, low], a_z.at[n], z_next),
            (part_z.at[0, n, high], b_z.at[n], z_prev),
            (part_z.at[1, n, high], up_z.at[n, high], z_next),
            (part_z.at[1, n, low], up_z.at[n, low], z_next),
            (part_z.at[2, n, low], down_z.at[n, low], z_prev),
            (part_z.at[2, n, high], down_z.at[n, high], z_prev),
            (mate_out.at[n], mate_in.at[n], y_mate),
        )[kind]
        return pltpu.make_async_remote_copy(
            src_ref=src, dst_ref=dst, send_sem=z_send.at[kind, n], recv_sem=z_recv.at[kind, n],
            device_id=peer, device_id_type=MESH,
        )

    mine = pl.ds(pl.multiple_of(y_lo * 64, 64), 64)
    theirs = pl.ds(pl.multiple_of(64 - y_lo * 64, 64), 64)

    def y_copy(kind, n):
        low, high = pl.ds(0, 32), pl.ds(32, 32)
        if kind < 4:
            src, dst, peer = part_y.at[kind, n, theirs], met_y.at[kind, n], y_mate
        else:
            src, dst, peer = (
                (sum_y.at[0, n, low], a_y.at[n], z_next),
                (sum_y.at[0, n, high], b_y.at[n], z_prev),
                (sum_y.at[1, n, high], up_y.at[n, high], z_next),
                (sum_y.at[1, n, low], up_y.at[n, low], z_next),
                (sum_y.at[2, n, low], down_y.at[n, low], z_prev),
                (sum_y.at[2, n, high], down_y.at[n, high], z_prev),
            )[kind - 4]
        return pltpu.make_async_remote_copy(
            src_ref=src, dst_ref=dst, send_sem=y_send.at[kind, n], recv_sem=y_recv.at[kind, n],
            device_id=peer, device_id_type=MESH,
        )

    def meet(t):
        for n in range(NY):
            y_copy(t, n).wait_recv()
            sum_y[t, n] = (part_y[t, n, mine].astype(f32) + met_y[t, n].astype(f32)).astype(bf16)
            for kind in ((4, 5), (6,), (8,))[t]:
                y_copy(kind, n).start()

    def add_far_z(t):
        for n in range(NZ):
            z_copy(t - 1, n).wait_recv()
            if t == 1:
                part_z[1, n, 0:64] = (part_z[1, n, 0:64].astype(f32) + a_z[n].astype(f32)).astype(bf16)
                z_copy(3, n).start()
            else:
                part_z[2, n, 64:128] = (part_z[2, n, 64:128].astype(f32) + b_z[n].astype(f32)).astype(bf16)
                z_copy(5, n).start()

    def add_far_y(t):
        for n in range(NY):
            y_copy(3 + t, n).wait_recv()
            if t == 1:
                sum_y[1, n, 0:32] = (sum_y[1, n, 0:32].astype(f32) + a_y[n].astype(f32)).astype(bf16)
                y_copy(7, n).start()
            else:
                sum_y[2, n, 32:64] = (sum_y[2, n, 32:64].astype(f32) + b_y[n].astype(f32)).astype(bf16)
                y_copy(9, n).start()

    for t in range(4):
        run(t * 4, 4, late)
        for g in range(4):
            state = acc[t * 4 + g]
            rows = state[0:128] / state[128:129]
            for j in range(2):
                head = 2 * g + j
                att[:, head * 128 : (head + 1) * 128] = rows[:, j * 128 : (j + 1) * 128].T.astype(bf16)

        for n in range(NY + NZ):
            piece = jnp.dot(
                att[...], w[:, n * PCOLS : (n + 1) * PCOLS], preferred_element_type=f32
            ).astype(bf16)
            if n < NY:
                part_y[t, n] = piece
            else:
                part_z[t, n - NY] = piece
            if n == NY - 1:
                for i in range(NY):
                    y_copy(t, i).start()
        for n in range(NZ):
            for kind in ((0, 1), (2,), (4,), ())[t]:
                z_copy(kind, n).start()
        if t > 0:
            meet(t - 1)
        if t > 1:
            add_far_z(t - 1)

    add_far_y(1)
    add_far_y(2)

    def total_z(n, rows):
        return (
            part_z[3, n, rows].astype(f32) + up_z[n, rows].astype(f32) + down_z[n, rows].astype(f32)
        )

    for n in range(NZ):
        for kind in (2, 3, 4, 5):
            z_copy(kind, n).wait_recv()
        mate_out[n] = total_z(n, theirs).astype(bf16)
        z_copy(6, n).start()

    for n in range(NY):
        for kind in (3, 6, 7, 8, 9):
            y_copy(kind, n).wait_recv()
        out_ref[:, n * PCOLS : (n + 1) * PCOLS] = (
            part_y[3, n, mine].astype(f32) + met_y[3, n].astype(f32)
            + up_y[n].astype(f32) + down_y[n].astype(f32)
        ).astype(bf16)

    for n in range(NZ):
        z_copy(6, n).wait_recv()
        out_ref[:, (NY + n) * PCOLS : (NY + n + 1) * PCOLS] = (
            total_z(n, mine) + mate_in[n].astype(f32)
        ).astype(bf16)

    for send in (0, 1, 2, 3, 6, 7, 8, 9):
        kv_copy(0, 0, send, sibling).wait_send()

    @pl.when(y_hi == 0)
    def _():
        for send in (4, 5):
            kv_copy(0, 0, send, sibling).wait_send()

    for n in range(NZ):
        for kind in range(7):
            z_copy(kind, n).wait_send()
    for n in range(NY):
        for kind in range(10):
            y_copy(kind, n).wait_send()


def on_device(queries, key_states, value_states, doc_ids, out_weight):
    vmem = pl.BlockSpec(memory_space=pltpu.VMEM)
    return pl.pallas_call(
        kernel,
        name="attend_project",
        out_shape=jax.ShapeDtypeStruct((64, D_OUT), bf16),
        in_specs=[pl.BlockSpec(memory_space=pl.ANY), vmem, vmem, vmem, pl.BlockSpec(memory_space=pl.ANY)],
        out_specs=vmem,
        scratch_shapes=[
            pltpu.VMEM((SLOTS + 2, BLOCK, 128), bf16),
            pltpu.VMEM((SLOTS, TOK, 128), bf16),
            pltpu.VMEM((UNITS, 256, 256), bf16),
            pltpu.VMEM((6 * TOK, 256), f32),
            pltpu.VMEM((6 * TOK, 256), f32),
            pltpu.VMEM((8, 256), f32),
            pltpu.VMEM((8, 256), f32),
            pltpu.VMEM((UNITS, 1, 256), f32),
            pltpu.VMEM((UNITS, VROWS, 256), f32),
            pltpu.VMEM((128, 1024), bf16),
            pltpu.VMEM((1024, D_OUT), bf16),
            pltpu.VMEM((4, NZ, 128, PCOLS), bf16),
            pltpu.VMEM((NZ, 64, PCOLS), bf16),
            pltpu.VMEM((NZ, 64, PCOLS), bf16),
            pltpu.VMEM((NZ, 128, PCOLS), bf16),
            pltpu.VMEM((NZ, 128, PCOLS), bf16),
            pltpu.VMEM((NZ, 64, PCOLS), bf16),
            pltpu.VMEM((NZ, 64, PCOLS), bf16),
            pltpu.VMEM((4, NY, 128, PCOLS), bf16),
            pltpu.VMEM((4, NY, 64, PCOLS), bf16),
            pltpu.VMEM((3, NY, 64, PCOLS), bf16),
            pltpu.VMEM((NY, 32, PCOLS), bf16),
            pltpu.VMEM((NY, 32, PCOLS), bf16),
            pltpu.VMEM((NY, 64, PCOLS), bf16),
            pltpu.VMEM((NY, 64, PCOLS), bf16),
            pltpu.SemaphoreType.DMA((10,)),
            pltpu.SemaphoreType.DMA((SLOTS + 2,)),
            pltpu.SemaphoreType.DMA((7, NZ)),
            pltpu.SemaphoreType.DMA((7, NZ)),
            pltpu.SemaphoreType.DMA((10, NY)),
            pltpu.SemaphoreType.DMA((10, NY)),
            pltpu.SemaphoreType.DMA,
            pltpu.VMEM((TOK, 1024), bf16),
            pltpu.SemaphoreType.DMA,
        ],
        compiler_params=pltpu.CompilerParams(
            collective_id=0, has_side_effects=True, vmem_limit_bytes=56 * 2**20
        ),
        cost_estimate=pl.CostEstimate(
            flops=14 * 10**9, bytes_accessed=10 * 2**20, transcendentals=19 * 10**6
        ),
    )(queries, key_states, value_states, doc_ids.reshape(4, 128), out_weight)


def solution(mesh):
    return jax.shard_map(
        on_device,
        mesh=mesh,
        in_specs=(P("ctx", "head"), P("ctx", "head"), P("ctx", "head"), P("ctx"), P("head", None)),
        out_specs=P(("ctx", "head"), None),
        check_vma=False,
    )
```

```python
import jax
import jax.numpy as jnp
from jax import lax
from jax.experimental import pallas as pl
from jax.experimental.pallas import tpu as pltpu
from jax.sharding import PartitionSpec as P

DH = 128
TOK = 512
VROWS = 144
BLOCK = TOK + 4 * VROWS
SLOTS = 9
RELAY_X, RELAY_Y = 9, 10
UNITS = 16
D_OUT = 4096
PCOLS = 512
NY, NZ = 4, 4
EXP_SCALE = DH**-0.5 * 1.4426950408889634
FAR = -1e30
MESH = pl.DeviceIdType.MESH
NT = (((1,), (1,)), ((), ()))
bf16 = jnp.bfloat16
f32 = jnp.float32


def kernel(
    q_hbm, k_ref, v_ref, ids_ref, w_hbm, out_ref,
    kv, kf, qx, s0, s1, mx0, mx1, top, acc, att, w,
    part_z, a_z, b_z, up_z, down_z, mate_out, mate_in,
    part_y, met_y, sum_y, far_y, near_y,
    kv_send, kv_recv, z_send, z_recv, y_send, y_recv, w_sem, q_ref, q_sem,
):
    c = lax.axis_index("ctx")
    h = lax.axis_index("head")
    x = c // 4
    y_hi = (c // 2) % 2
    core = c % 2
    y_lo = h // 4
    z = h % 4

    def at_x(step):
        return (((x + step) % 4) * 4 + y_hi * 2 + core, h)

    def at_z(step):
        return (c, y_lo * 4 + (z + step) % 4)

    x_next, x_prev, x_far = at_x(1), at_x(3), at_x(2)
    y_pair = (x * 4 + (1 - y_hi) * 2 + core, h)
    sibling = (x * 4 + y_hi * 2 + 1 - core, h)
    z_next, z_prev = at_z(1), at_z(3)
    y_mate = (c, (1 - y_lo) * 4 + z)

    barrier = pltpu.get_barrier_semaphore()
    for peer in (x_next, x_prev, x_far, y_pair, sibling, z_next, z_prev, y_mate):
        pl.semaphore_signal(barrier, inc=1, device_id=peer, device_id_type=MESH)

    q_copy = pltpu.make_async_copy(q_hbm, q_ref, q_sem)
    q_copy.start()
    w_copy = pltpu.make_async_copy(w_hbm, w, w_sem)
    w_copy.start()

    kv[0, 0:TOK, :] = k_ref[...]
    sub16 = lax.broadcasted_iota(jnp.int32, (16, 128), 0)
    for r in range(4):
        base = TOK + r * VROWS
        kv[0, base : base + 128, :] = (
            v_ref[r * 128 : (r + 1) * 128, :].astype(f32).T.astype(bf16)
        )
        id_row = jnp.broadcast_to(ids_ref[r : r + 1, :].astype(f32), (16, 128))
        kv[0, base + 128 : base + VROWS, :] = jnp.where(
            sub16 == 0, 1.0, jnp.where(sub16 == 1, id_row, 0.0)
        ).astype(bf16)

    pl.semaphore_wait(barrier, 8)

    def kv_copy(src, dst, send, peer):
        return pltpu.make_async_remote_copy(
            src_ref=kv.at[src],
            dst_ref=kv.at[dst],
            send_sem=kv_send.at[send],
            recv_sem=kv_recv.at[dst],
            device_id=peer,
            device_id_type=MESH,
        )

    def arrived(slot):
        kv_copy(slot, slot, 0, sibling).wait_recv()

    @pl.when(y_hi == 0)
    def _():
        kv_copy(0, 4, 0, x_next).start()
        kv_copy(0, 2, 1, y_pair).start()
        kv_copy(0, RELAY_X, 2, x_prev).start()

    @pl.when(y_hi == 1)
    def _():
        kv_copy(0, 8, 0, x_far).start()
        kv_copy(0, RELAY_Y, 1, y_pair).start()

    def share(slot):
        @pl.when(core == 0)
        def _():
            if slot < 8:
                kv_copy(slot, slot + 1, 6 + slot // 2, sibling).start()

        @pl.when(core == 1)
        def _():
            if slot > 0:
                kv_copy(slot, slot - 1, 5 + slot // 2, sibling).start()

    share(0)

    lane = lax.broadcasted_iota(jnp.int32, (128, 128), 1).astype(f32)

    def id_columns(slot, r):
        base = TOK + r * VROWS + 128
        row = kv[slot, base : base + 16, :].astype(f32)[1:2, :]
        return jnp.broadcast_to(row, (128, 128)).T

    def key_marks(slot):
        shift = jnp.where(c >= slot, 0.0, 1000.0)
        for r in range(4):
            kf[slot, r * 128 : (r + 1) * 128, :] = jnp.where(
                id_columns(slot, r) + shift == lane, 0.0, FAR
            ).astype(bf16)

    order = ((2, 2), (3, 1), (1, 3), (0, 0))
    firsts = [(((z + low) % 4) * 64, ((z + high) % 4) * 64 + 256) for low, high in order]

    q_copy.wait()

    for r in range(4):
        kf[0, r * 128 : (r + 1) * 128, :] = jnp.where(id_columns(0, r) == lane, 1.0, 0.0).astype(bf16)
    for t in range(4):
        for half in range(2):
            rows = pl.ds(pl.multiple_of(firsts[t][half], 64), 64)
            marks = kf[0, rows, :]
            for g in range(4):
                for j in range(2):
                    place = j * 128 + half * 64
                    head = 2 * g + j
                    qx[t * 4 + g, place : place + 64, 0:128] = q_ref[rows, head * 128 : (head + 1) * 128]
                    qx[t * 4 + g, place : place + 64, 128:256] = marks
    key_marks(0)

    key_index = lax.broadcasted_iota(jnp.int32, (TOK, 256), 0)
    lane_q = lax.broadcasted_iota(jnp.int32, (1, 256), 1) % 128

    def score(unit, slot, i, s_ref, diagonal):
        keys = jnp.concatenate([kv[slot, 0:TOK, :], kf[slot]], axis=1)
        s = lax.dot_general(keys, qx[unit], NT, preferred_element_type=f32)
        if diagonal:
            t = unit // 4
            low = jnp.where(t == 0, 2, jnp.where(t == 1, 3, jnp.where(t == 2, 1, 0)))
            high = jnp.where(t == 0, 2, jnp.where(t == 1, 1, jnp.where(t == 2, 3, 0)))
            low_first = ((z + low) % 4) * 64
            high_first = ((z + high) % 4) * 64 + 192
            q_index = lane_q + jnp.where(lane_q < 64, low_first, high_first)
            s = jnp.where(key_index <= q_index, s, FAR)
        s_ref[i * TOK : (i + 1) * TOK, :] = s
        return jnp.max(s.reshape(TOK // 8, 8, 256), axis=0)

    def weigh(slot, i, s_ref, new_top):
        values = jnp.concatenate(
            [kv[slot, TOK + r * VROWS : TOK + (r + 1) * VROWS, :] for r in range(4)], axis=1
        )
        probs = jnp.exp2((s_ref[i * TOK : (i + 1) * TOK, :] - new_top) * EXP_SCALE).astype(bf16)
        return jnp.dot(values, probs, preferred_element_type=f32)

    def stage(ahead, now, slots, into, held, diagonal):
        if now is not None:
            new_top = jnp.max(held[1][...], axis=0, keepdims=True)
            if not diagonal:
                old_top = top[now]
                new_top = jnp.maximum(old_top, new_top)
        highest, add = None, None
        for i, slot in enumerate(slots):
            if ahead is not None:
                here = score(ahead, slot, i, into[0], diagonal)
                highest = here if highest is None else jnp.maximum(highest, here)
            if now is not None:
                here = weigh(slot, i, held[0], new_top)
                add = here if add is None else add + here
        if ahead is not None:
            into[1][...] = highest
        if now is not None:
            if diagonal:
                acc[now] = add
            else:
                acc[now] = acc[now] * jnp.exp2((old_top - new_top) * EXP_SCALE) + add
            top[now] = new_top

    pair = ((s0, mx0), (s1, mx1))

    def run(first, count, slots, diagonal=False):
        stage(first, None, slots, pair[0], None, diagonal)

        def body(i, carry):
            for e in range(4):
                now = first + 4 * i + e
                ahead = now + 1
                if e == 3:
                    ahead = None if count == 4 else jnp.minimum(ahead, first + count - 1)
                stage(ahead, now, slots, pair[(e + 1) % 2], pair[e % 2], diagonal)
            return carry

        if count == 4:
            body(0, 0)
        else:
            lax.fori_loop(0, count // 4, body, 0)

    run(0, UNITS, (0,), True)

    @pl.when(y_hi == 0)
    def _():
        arrived(4)
        kv_copy(4, 6, 3, y_pair).start()
        share(4)
        arrived(RELAY_X)
        kv_copy(RELAY_X, 8, 4, x_prev).start()
        arrived(RELAY_Y)
        kv_copy(RELAY_Y, 2, 5, x_next).start()

    @pl.when(y_hi == 1)
    def _():
        arrived(8)
        kv_copy(8, 6, 3, y_pair).start()
        kv_copy(0, 4, 2, x_next).start()
        share(8)
        arrived(2)
        share(2)

    early = (4 + 4 * y_hi, 2 * y_hi + (1 - y_hi) * (3 + 2 * core))
    late = (
        2 - y_hi, 6 - 2 * y_hi, 8 - 2 * y_hi, 1 + 2 * y_hi, 5 - 2 * core * (1 - y_hi), 7,
    )
    key_marks(early[0])

    @pl.when(y_hi == 0)
    def _():
        @pl.when(core == 0)
        def _():
            arrived(3)

        @pl.when(core == 1)
        def _():
            arrived(5)

    key_marks(early[1])
    run(0, UNITS, early)

    @pl.when(y_hi == 0)
    def _():
        arrived(2)
        share(2)
        arrived(6)
        share(6)
        arrived(8)
        share(8)

    @pl.when(y_hi == 1)
    def _():
        arrived(4)
        share(4)
        arrived(6)
        share(6)
        arrived(1)

    for slot in late[:3]:
        key_marks(slot)

    def arrive_last():
        @pl.when(y_hi == 0)
        def _():
            arrived(1)

            @pl.when(core == 0)
            def _():
                arrived(5)

            @pl.when(core == 1)
            def _():
                arrived(3)

        @pl.when(y_hi == 1)
        def _():
            arrived(3)
            arrived(5)

        arrived(7)
        for slot in late[3:]:
            key_marks(slot)

    w_copy.wait()

    def z_copy(kind, n):
        low, high = pl.ds(0, 64), pl.ds(64, 64)
        src, dst, peer = (
            (part_z.at[0, n, low], a_z.at[n], z_next),
            (part_z.at[0, n, high], b_z.at[n], z_prev),
            (part_z.at[1, n, high], up_z.at[n, high], z_next),
            (part_z.at[2, n, low], up_z.at[n, low], z_next),
            (part_z.at[1, n, low], down_z.at[n, low], z_prev),
            (part_z.at[2, n, high], down_z.at[n, high], z_prev),
            (mate_out.at[n], mate_in.at[n], y_mate),
        )[kind]
        return pltpu.make_async_remote_copy(
            src_ref=src, dst_ref=dst, send_sem=z_send.at[kind, n], recv_sem=z_recv.at[kind, n],
            device_id=peer, device_id_type=MESH,
        )

    mine = pl.ds(pl.multiple_of(y_lo * 64, 64), 64)
    theirs = pl.ds(pl.multiple_of(64 - y_lo * 64, 64), 64)

    def way(t):
        return (t + y_lo) % 2

    def half_of(t, with_far):
        first = 32 * way(t) if with_far else 32 - 32 * way(t)
        return pl.ds(pl.multiple_of(first, 32), 32)

    def y_copy(kind, n):
        place = kind
        if kind < 4:
            src, dst, peer = part_y.at[kind, n, theirs], met_y.at[kind, n], y_mate
        elif kind < 6:
            src = sum_y.at[0, n, pl.ds(32 * (kind - 4), 32)]
            dst, peer = far_y.at[kind - 4, n], (z_next, z_prev)[kind - 4]
        else:
            t, with_far = kind // 2 - 2, kind % 2
            rows = half_of(t, with_far)
            src, dst, peer = sum_y.at[t, n, rows], near_y.at[way(t), n, rows], at_z(1 + 2 * way(t))
            place = 6 + 2 * way(t) + with_far
        return pltpu.make_async_remote_copy(
            src_ref=src, dst_ref=dst, send_sem=y_send.at[kind, n], recv_sem=y_recv.at[place, n],
            device_id=peer, device_id_type=MESH,
        )

    def meet(t):
        for n in range(NY):
            y_copy(t, n).wait_recv()
            sum_y[t, n] = (part_y[t, n, mine].astype(f32) + met_y[t, n].astype(f32)).astype(bf16)
            for kind in ((4, 5), (6,), (8,))[t]:
                y_copy(kind, n).start()

    def add_far_z():
        for n in range(NZ):
            z_copy(0, n).wait_recv()
            part_z[2, n, 0:64] = (part_z[2, n, 0:64].astype(f32) + a_z[n].astype(f32)).astype(bf16)
            z_copy(3, n).start()
            z_copy(1, n).wait_recv()
            part_z[2, n, 64:128] = (part_z[2, n, 64:128].astype(f32) + b_z[n].astype(f32)).astype(bf16)
            z_copy(5, n).start()

    def add_far_y():
        for n in range(NY):
            y_copy(4, n).wait_recv()
            y_copy(5, n).wait_recv()
            for t in (1, 2):
                rows = half_of(t, 1)
                sum_y[t, n, rows] = (
                    sum_y[t, n, rows].astype(f32) + far_y[way(t), n].astype(f32)
                ).astype(bf16)
                y_copy(5 + 2 * t, n).start()

    for t in range(4):
        if t == 0:
            run(0, 4, late[:3])
            arrive_last()
            run(0, 4, late[3:])
        else:
            run(t * 4, 4, late)
        for g in range(4):
            state = acc[t * 4 + g]
            rows = state[0:128] / state[128:129]
            for j in range(2):
                head = 2 * g + j
                att[:, head * 128 : (head + 1) * 128] = rows[:, j * 128 : (j + 1) * 128].T.astype(bf16)

        for n in range(NY + NZ):
            piece = jnp.dot(
                att[...], w[:, n * PCOLS : (n + 1) * PCOLS], preferred_element_type=f32
            ).astype(bf16)
            if n < NY:
                part_y[t, n] = piece
            else:
                part_z[t, n - NY] = piece
            if n == NY - 1:
                for i in range(NY):
                    y_copy(t, i).start()
        for n in range(NZ):
            for kind in ((0, 1), (2, 4), (), ())[t]:
                z_copy(kind, n).start()
        if t > 0:
            meet(t - 1)
        if t == 2:
            add_far_z()

    add_far_y()

    def total_z(n, rows):
        return (
            part_z[3, n, rows].astype(f32) + up_z[n, rows].astype(f32) + down_z[n, rows].astype(f32)
        )

    for n in range(NZ):
        for kind in (2, 3, 4, 5):
            z_copy(kind, n).wait_recv()
        mate_out[n] = total_z(n, theirs).astype(bf16)
        z_copy(6, n).start()

    for n in range(NY):
        for kind in (3, 6, 7, 8, 9):
            y_copy(kind, n).wait_recv()
        out_ref[:, n * PCOLS : (n + 1) * PCOLS] = (
            part_y[3, n, mine].astype(f32) + met_y[3, n].astype(f32)
            + near_y[0, n].astype(f32) + near_y[1, n].astype(f32)
        ).astype(bf16)

    for n in range(NZ):
        z_copy(6, n).wait_recv()
        out_ref[:, (NY + n) * PCOLS : (NY + n + 1) * PCOLS] = (
            total_z(n, mine) + mate_in[n].astype(f32)
        ).astype(bf16)

    for send in (0, 1, 2, 3, 6, 7, 8, 9):
        kv_copy(0, 0, send, sibling).wait_send()

    @pl.when(y_hi == 0)
    def _():
        for send in (4, 5):
            kv_copy(0, 0, send, sibling).wait_send()

    for n in range(NZ):
        for kind in range(7):
            z_copy(kind, n).wait_send()
    for n in range(NY):
        for kind in range(10):
            y_copy(kind, n).wait_send()


def on_device(queries, key_states, value_states, doc_ids, out_weight):
    vmem = pl.BlockSpec(memory_space=pltpu.VMEM)
    return pl.pallas_call(
        kernel,
        name="attend_project",
        out_shape=jax.ShapeDtypeStruct((64, D_OUT), bf16),
        in_specs=[pl.BlockSpec(memory_space=pl.ANY), vmem, vmem, vmem, pl.BlockSpec(memory_space=pl.ANY)],
        out_specs=vmem,
        scratch_shapes=[
            pltpu.VMEM((SLOTS + 2, BLOCK, 128), bf16),
            pltpu.VMEM((SLOTS, TOK, 128), bf16),
            pltpu.VMEM((UNITS, 256, 256), bf16),
            pltpu.VMEM((6 * TOK, 256), f32),
            pltpu.VMEM((6 * TOK, 256), f32),
            pltpu.VMEM((8, 256), f32),
            pltpu.VMEM((8, 256), f32),
            pltpu.VMEM((UNITS, 1, 256), f32),
            pltpu.VMEM((UNITS, VROWS, 256), f32),
            pltpu.VMEM((128, 1024), bf16),
            pltpu.VMEM((1024, D_OUT), bf16),
            pltpu.VMEM((4, NZ, 128, PCOLS), bf16),
            pltpu.VMEM((NZ, 64, PCOLS), bf16),
            pltpu.VMEM((NZ, 64, PCOLS), bf16),
            pltpu.VMEM((NZ, 128, PCOLS), bf16),
            pltpu.VMEM((NZ, 128, PCOLS), bf16),
            pltpu.VMEM((NZ, 64, PCOLS), bf16),
            pltpu.VMEM((NZ, 64, PCOLS), bf16),
            pltpu.VMEM((4, NY, 128, PCOLS), bf16),
            pltpu.VMEM((4, NY, 64, PCOLS), bf16),
            pltpu.VMEM((3, NY, 64, PCOLS), bf16),
            pltpu.VMEM((2, NY, 32, PCOLS), bf16),
            pltpu.VMEM((2, NY, 64, PCOLS), bf16),
            pltpu.SemaphoreType.DMA((10,)),
            pltpu.SemaphoreType.DMA((SLOTS + 2,)),
            pltpu.SemaphoreType.DMA((7, NZ)),
            pltpu.SemaphoreType.DMA((7, NZ)),
            pltpu.SemaphoreType.DMA((10, NY)),
            pltpu.SemaphoreType.DMA((10, NY)),
            pltpu.SemaphoreType.DMA,
            pltpu.VMEM((TOK, 1024), bf16),
            pltpu.SemaphoreType.DMA,
        ],
        compiler_params=pltpu.CompilerParams(
            collective_id=0, has_side_effects=True, vmem_limit_bytes=56 * 2**20
        ),
        cost_estimate=pl.CostEstimate(
            flops=14 * 10**9, bytes_accessed=10 * 2**20, transcendentals=19 * 10**6
        ),
    )(queries, key_states, value_states, doc_ids.reshape(4, 128), out_weight)


def solution(mesh):
    return jax.shard_map(
        on_device,
        mesh=mesh,
        in_specs=(P("ctx", "head"), P("ctx", "head"), P("ctx", "head"), P("ctx"), P("head", None)),
        out_specs=P(("ctx", "head"), None),
        check_vma=False,
    )
```

```python
import jax
import jax.numpy as jnp
from jax import lax
from jax.experimental import pallas as pl
from jax.experimental.pallas import tpu as pltpu
from jax.sharding import PartitionSpec as P

DH = 128
TOK = 512
VROWS = 144
IDS = 2 * TOK
BLOCK = IDS + 16
SLOTS = 9
RELAY_X, RELAY_Y = 9, 10
UNITS = 16
D_OUT = 4096
PCOLS = 512
NY, NZ = 4, 4
EXP_SCALE = DH**-0.5 * 1.4426950408889634
FAR = -1e30
MESH = pl.DeviceIdType.MESH
NT = (((1,), (1,)), ((), ()))
bf16 = jnp.bfloat16
f32 = jnp.float32


def kernel(
    q_hbm, k_hbm, v_hbm, ids_hbm, w_hbm, one_ref, two_ref,
    kv, kf, qx, s0, s1, mx0, mx1, top, acc, att, w,
    part_z, a_z, b_z, up_z, down_z, mate_out, mate_in,
    part_y, met_y, sum_y, far_y, near_y,
    kv_send, kv_recv, z_send, z_recv, y_send, y_recv, w_sem, q_ref, v_ref, ids_ref, in_sem,
):
    c = lax.axis_index("ctx")
    h = lax.axis_index("head")
    x = c // 4
    y_hi = (c // 2) % 2
    core = c % 2
    y_lo = h // 4
    z = h % 4

    def at_x(step):
        return (((x + step) % 4) * 4 + y_hi * 2 + core, h)

    def at_z(step):
        return (c, y_lo * 4 + (z + step) % 4)

    x_next, x_prev, x_far = at_x(1), at_x(3), at_x(2)
    y_pair = (x * 4 + (1 - y_hi) * 2 + core, h)
    sibling = (x * 4 + y_hi * 2 + 1 - core, h)
    z_next, z_prev = at_z(1), at_z(3)
    y_mate = (c, (1 - y_lo) * 4 + z)

    ids_copy = pltpu.make_async_copy(ids_hbm, ids_ref, in_sem.at[0])
    ids_copy.start()
    v_copy = pltpu.make_async_copy(v_hbm, v_ref, in_sem.at[1])
    v_copy.start()
    k_copy = pltpu.make_async_copy(k_hbm, kv.at[0, pl.ds(0, TOK)], in_sem.at[2])
    k_copy.start()
    q_copy = pltpu.make_async_copy(q_hbm, q_ref, in_sem.at[3])
    q_copy.start()
    w_copy = pltpu.make_async_copy(w_hbm, w, w_sem)
    w_copy.start()

    barrier = pltpu.get_barrier_semaphore()
    for peer in (x_next, x_prev, x_far, y_pair, sibling, z_next, z_prev, y_mate):
        pl.semaphore_signal(barrier, inc=1, device_id=peer, device_id_type=MESH)

    ids_copy.wait()
    kv[0, IDS:BLOCK, :] = jnp.concatenate(
        [ids_ref[...].astype(f32), jnp.zeros((12, 128), f32)], axis=0
    ).astype(bf16)
    v_copy.wait()
    for r in range(4):
        kv[0, TOK + r * 128 : TOK + (r + 1) * 128, :] = (
            v_ref[r * 128 : (r + 1) * 128, :].astype(f32).T.astype(bf16)
        )
    k_copy.wait()

    pl.semaphore_wait(barrier, 8)

    def kv_copy(src, dst, send, peer):
        return pltpu.make_async_remote_copy(
            src_ref=kv.at[src],
            dst_ref=kv.at[dst],
            send_sem=kv_send.at[send],
            recv_sem=kv_recv.at[dst],
            device_id=peer,
            device_id_type=MESH,
        )

    def arrived(slot):
        kv_copy(slot, slot, 0, sibling).wait_recv()

    @pl.when(y_hi == 0)
    def _():
        kv_copy(0, 4, 0, x_next).start()
        kv_copy(0, 2, 1, y_pair).start()
        kv_copy(0, RELAY_X, 2, x_prev).start()

    @pl.when(y_hi == 1)
    def _():
        kv_copy(0, 8, 0, x_far).start()
        kv_copy(0, RELAY_Y, 1, y_pair).start()

    def share(slot):
        @pl.when(core == 0)
        def _():
            if slot < 8:
                kv_copy(slot, slot + 1, 6 + slot // 2, sibling).start()

        @pl.when(core == 1)
        def _():
            if slot > 0:
                kv_copy(slot, slot - 1, 5 + slot // 2, sibling).start()

    share(0)

    lane = lax.broadcasted_iota(jnp.int32, (128, 128), 1).astype(f32)

    def id_columns(slot, r):
        row = kv[slot, IDS:BLOCK, :].astype(f32)[r : r + 1, :]
        return jnp.broadcast_to(row, (128, 128)).T

    def key_marks(slot):
        shift = jnp.where(c >= slot, 0.0, 1000.0)
        for r in range(4):
            kf[slot, r * 128 : (r + 1) * 128, :] = jnp.where(
                id_columns(slot, r) + shift == lane, 0.0, FAR
            ).astype(bf16)

    order = ((2, 2), (3, 1), (1, 3), (0, 0))
    firsts = [(((z + low) % 4) * 64, ((z + high) % 4) * 64 + 256) for low, high in order]

    q_copy.wait()

    for r in range(4):
        kf[0, r * 128 : (r + 1) * 128, :] = jnp.where(id_columns(0, r) == lane, 1.0, 0.0).astype(bf16)
    for t in range(4):
        for half in range(2):
            rows = pl.ds(pl.multiple_of(firsts[t][half], 64), 64)
            marks = kf[0, rows, :]
            for g in range(4):
                for j in range(2):
                    place = j * 128 + half * 64
                    head = 2 * g + j
                    qx[t * 4 + g, place : place + 64, 0:128] = q_ref[rows, head * 128 : (head + 1) * 128]
                    qx[t * 4 + g, place : place + 64, 128:256] = marks
    key_marks(0)

    ones = jnp.ones((VROWS - 128, TOK), bf16)
    key_index = lax.broadcasted_iota(jnp.int32, (TOK, 256), 0)
    lane_q = lax.broadcasted_iota(jnp.int32, (1, 256), 1) % 128

    def score(unit, slot, i, s_ref, diagonal):
        keys = jnp.concatenate([kv[slot, 0:TOK, :], kf[slot]], axis=1)
        s = lax.dot_general(keys, qx[unit], NT, preferred_element_type=f32)
        if diagonal:
            t = unit // 4
            low = jnp.where(t == 0, 2, jnp.where(t == 1, 3, jnp.where(t == 2, 1, 0)))
            high = jnp.where(t == 0, 2, jnp.where(t == 1, 1, jnp.where(t == 2, 3, 0)))
            low_first = ((z + low) % 4) * 64
            high_first = ((z + high) % 4) * 64 + 192
            q_index = lane_q + jnp.where(lane_q < 64, low_first, high_first)
            s = jnp.where(key_index <= q_index, s, FAR)
        s_ref[i * TOK : (i + 1) * TOK, :] = s
        return jnp.max(s.reshape(TOK // 8, 8, 256), axis=0)

    def weigh(slot, i, s_ref, new_top):
        values = jnp.concatenate(
            [kv[slot, TOK + r * 128 : TOK + (r + 1) * 128, :] for r in range(4)], axis=1
        )
        values = jnp.concatenate([values, ones], axis=0)
        probs = jnp.exp2((s_ref[i * TOK : (i + 1) * TOK, :] - new_top) * EXP_SCALE).astype(bf16)
        return jnp.dot(values, probs, preferred_element_type=f32)

    def stage(ahead, now, slots, into, held, diagonal):
        if now is not None:
            new_top = jnp.max(held[1][...], axis=0, keepdims=True)
            if not diagonal:
                old_top = top[now]
                new_top = jnp.maximum(old_top, new_top)
        highest, add = None, None
        for i, slot in enumerate(slots):
            if ahead is not None:
                here = score(ahead, slot, i, into[0], diagonal)
                highest = here if highest is None else jnp.maximum(highest, here)
            if now is not None:
                here = weigh(slot, i, held[0], new_top)
                add = here if add is None else add + here
        if ahead is not None:
            into[1][...] = highest
        if now is not None:
            if diagonal:
                acc[now] = add
            else:
                acc[now] = acc[now] * jnp.exp2((old_top - new_top) * EXP_SCALE) + add
            top[now] = new_top

    pair = ((s0, mx0), (s1, mx1))

    def run(first, count, slots, diagonal=False):
        stage(first, None, slots, pair[0], None, diagonal)

        def body(i, carry):
            for e in range(4):
                now = first + 4 * i + e
                ahead = now + 1
                if e == 3:
                    ahead = None if count == 4 else jnp.minimum(ahead, first + count - 1)
                stage(ahead, now, slots, pair[(e + 1) % 2], pair[e % 2], diagonal)
            return carry

        if count == 4:
            body(0, 0)
        else:
            lax.fori_loop(0, count // 4, body, 0)

    run(0, UNITS, (0,), True)

    @pl.when(y_hi == 0)
    def _():
        arrived(4)
        kv_copy(4, 6, 3, y_pair).start()
        share(4)
        arrived(RELAY_X)
        kv_copy(RELAY_X, 8, 4, x_prev).start()
        arrived(RELAY_Y)
        kv_copy(RELAY_Y, 2, 5, x_next).start()

    @pl.when(y_hi == 1)
    def _():
        arrived(8)
        kv_copy(8, 6, 3, y_pair).start()
        kv_copy(0, 4, 2, x_next).start()
        share(8)
        arrived(2)
        share(2)

    early = (4 + 4 * y_hi, 2 * y_hi + (1 - y_hi) * (3 + 2 * core))
    late = (
        2 - y_hi, 6 - 2 * y_hi, 8 - 2 * y_hi, 1 + 2 * y_hi, 5 - 2 * core * (1 - y_hi), 7,
    )
    key_marks(early[0])

    @pl.when(y_hi == 0)
    def _():
        @pl.when(core == 0)
        def _():
            arrived(3)

        @pl.when(core == 1)
        def _():
            arrived(5)

    key_marks(early[1])
    run(0, UNITS, early)

    @pl.when(y_hi == 0)
    def _():
        arrived(2)
        share(2)
        arrived(6)
        share(6)
        arrived(8)
        share(8)

    @pl.when(y_hi == 1)
    def _():
        arrived(4)
        share(4)
        arrived(6)
        share(6)
        arrived(1)

    for slot in late[:3]:
        key_marks(slot)

    def arrive_last():
        @pl.when(y_hi == 0)
        def _():
            arrived(1)

            @pl.when(core == 0)
            def _():
                arrived(5)

            @pl.when(core == 1)
            def _():
                arrived(3)

        @pl.when(y_hi == 1)
        def _():
            arrived(3)
            arrived(5)

        arrived(7)
        for slot in late[3:]:
            key_marks(slot)

    w_copy.wait()

    def z_copy(kind, n):
        low, high = pl.ds(0, 64), pl.ds(64, 64)
        src, dst, peer = (
            (part_z.at[0, n, low], a_z.at[n], z_next),
            (part_z.at[0, n, high], b_z.at[n], z_prev),
            (part_z.at[1, n, high], up_z.at[n, high], z_next),
            (part_z.at[2, n, low], up_z.at[n, low], z_next),
            (part_z.at[1, n, low], down_z.at[n, low], z_prev),
            (part_z.at[2, n, high], down_z.at[n, high], z_prev),
            (mate_out.at[n], mate_in.at[n], y_mate),
        )[kind]
        return pltpu.make_async_remote_copy(
            src_ref=src, dst_ref=dst, send_sem=z_send.at[kind, n], recv_sem=z_recv.at[kind, n],
            device_id=peer, device_id_type=MESH,
        )

    mine = pl.ds(pl.multiple_of(y_lo * 64, 64), 64)
    theirs = pl.ds(pl.multiple_of(64 - y_lo * 64, 64), 64)

    def way(t):
        return (t + y_lo) % 2

    def half_of(t, with_far):
        first = 32 * way(t) if with_far else 32 - 32 * way(t)
        return pl.ds(pl.multiple_of(first, 32), 32)

    def y_copy(kind, n):
        place = kind
        if kind < 4:
            src, dst, peer = part_y.at[kind, n, theirs], met_y.at[kind, n], y_mate
        elif kind < 6:
            src = sum_y.at[0, n, pl.ds(32 * (kind - 4), 32)]
            dst, peer = far_y.at[kind - 4, n], (z_next, z_prev)[kind - 4]
        else:
            t, with_far = kind // 2 - 2, kind % 2
            rows = half_of(t, with_far)
            src, dst, peer = sum_y.at[t, n, rows], near_y.at[way(t), n, rows], at_z(1 + 2 * way(t))
            place = 6 + 2 * way(t) + with_far
        return pltpu.make_async_remote_copy(
            src_ref=src, dst_ref=dst, send_sem=y_send.at[kind, n], recv_sem=y_recv.at[place, n],
            device_id=peer, device_id_type=MESH,
        )

    def meet(t):
        for n in range(NY):
            y_copy(t, n).wait_recv()
            sum_y[t, n] = (part_y[t, n, mine].astype(f32) + met_y[t, n].astype(f32)).astype(bf16)
            for kind in ((4, 5), (6,), (8,))[t]:
                y_copy(kind, n).start()

    def add_far_z():
        for n in range(NZ):
            z_copy(0, n).wait_recv()
            part_z[2, n, 0:64] = (part_z[2, n, 0:64].astype(f32) + a_z[n].astype(f32)).astype(bf16)
            z_copy(3, n).start()
            z_copy(1, n).wait_recv()
            part_z[2, n, 64:128] = (part_z[2, n, 64:128].astype(f32) + b_z[n].astype(f32)).astype(bf16)
            z_copy(5, n).start()

    def add_far_y():
        for n in range(NY):
            y_copy(4, n).wait_recv()
            y_copy(5, n).wait_recv()
            for t in (1, 2):
                rows = half_of(t, 1)
                sum_y[t, n, rows] = (
                    sum_y[t, n, rows].astype(f32) + far_y[way(t), n].astype(f32)
                ).astype(bf16)
                y_copy(5 + 2 * t, n).start()

    for t in range(4):
        if t == 0:
            run(0, 4, late[:3])
            arrive_last()
            run(0, 4, late[3:])
        else:
            run(t * 4, 4, late)
        for g in range(4):
            state = acc[t * 4 + g]
            rows = state[0:128] / state[128:129]
            for j in range(2):
                head = 2 * g + j
                att[:, head * 128 : (head + 1) * 128] = rows[:, j * 128 : (j + 1) * 128].T.astype(bf16)

        for n in range(NY + NZ):
            piece = jnp.dot(
                att[...], w[:, n * PCOLS : (n + 1) * PCOLS], preferred_element_type=f32
            ).astype(bf16)
            if n < NY:
                part_y[t, n] = piece
            else:
                part_z[t, n - NY] = piece
            if n == NY - 1:
                for i in range(NY):
                    y_copy(t, i).start()
            if n == NY + 1 or n == NY + 3:
                for i in (n - NY - 1, n - NY):
                    for kind in ((0, 1), (2, 4), (), ())[t]:
                        z_copy(kind, i).start()
        if t > 0:
            meet(t - 1)
        if t == 2:
            add_far_z()

    add_far_y()

    def total_z(n, rows):
        return (
            part_z[3, n, rows].astype(f32) + up_z[n, rows].astype(f32) + down_z[n, rows].astype(f32)
        )

    for n in range(NZ):
        for kind in (2, 3, 4, 5):
            z_copy(kind, n).wait_recv()
        mate_out[n] = total_z(n, theirs).astype(bf16)
        z_copy(6, n).start()

    for n in range(NZ):
        one_ref[:, (NY + n) * PCOLS : (NY + n + 1) * PCOLS] = total_z(n, mine).astype(bf16)

    for n in range(NY):
        y_copy(3, n).wait_recv()
        one_ref[:, n * PCOLS : (n + 1) * PCOLS] = (
            part_y[3, n, mine].astype(f32) + met_y[3, n].astype(f32)
        ).astype(bf16)

    for n in range(NY):
        for kind in (6, 7, 8, 9):
            y_copy(kind, n).wait_recv()
        two_ref[:, n * PCOLS : (n + 1) * PCOLS] = (
            near_y[0, n].astype(f32) + near_y[1, n].astype(f32)
        ).astype(bf16)

    for n in range(NZ):
        z_copy(6, n).wait_recv()
        two_ref[:, (NY + n) * PCOLS : (NY + n + 1) * PCOLS] = mate_in[n]

    for send in (0, 1, 2, 3, 6, 7, 8, 9):
        kv_copy(0, 0, send, sibling).wait_send()

    @pl.when(y_hi == 0)
    def _():
        for send in (4, 5):
            kv_copy(0, 0, send, sibling).wait_send()

    for n in range(NZ):
        for kind in range(7):
            z_copy(kind, n).wait_send()
    for n in range(NY):
        for kind in range(10):
            y_copy(kind, n).wait_send()


def on_device(queries, key_states, value_states, doc_ids, out_weight):
    vmem = pl.BlockSpec(memory_space=pltpu.VMEM)
    one, two = pl.pallas_call(
        kernel,
        name="attend_project",
        out_shape=[jax.ShapeDtypeStruct((64, D_OUT), bf16)] * 2,
        in_specs=[pl.BlockSpec(memory_space=pl.ANY)] * 5,
        out_specs=[vmem, vmem],
        scratch_shapes=[
            pltpu.VMEM((SLOTS + 2, BLOCK, 128), bf16),
            pltpu.VMEM((SLOTS, TOK, 128), bf16),
            pltpu.VMEM((UNITS, 256, 256), bf16),
            pltpu.VMEM((6 * TOK, 256), f32),
            pltpu.VMEM((6 * TOK, 256), f32),
            pltpu.VMEM((8, 256), f32),
            pltpu.VMEM((8, 256), f32),
            pltpu.VMEM((UNITS, 1, 256), f32),
            pltpu.VMEM((UNITS, VROWS, 256), f32),
            pltpu.VMEM((128, 1024), bf16),
            pltpu.VMEM((1024, D_OUT), bf16),
            pltpu.VMEM((4, NZ, 128, PCOLS), bf16),
            pltpu.VMEM((NZ, 64, PCOLS), bf16),
            pltpu.VMEM((NZ, 64, PCOLS), bf16),
            pltpu.VMEM((NZ, 128, PCOLS), bf16),
            pltpu.VMEM((NZ, 128, PCOLS), bf16),
            pltpu.VMEM((NZ, 64, PCOLS), bf16),
            pltpu.VMEM((NZ, 64, PCOLS), bf16),
            pltpu.VMEM((4, NY, 128, PCOLS), bf16),
            pltpu.VMEM((4, NY, 64, PCOLS), bf16),
            pltpu.VMEM((3, NY, 64, PCOLS), bf16),
            pltpu.VMEM((2, NY, 32, PCOLS), bf16),
            pltpu.VMEM((2, NY, 64, PCOLS), bf16),
            pltpu.SemaphoreType.DMA((10,)),
            pltpu.SemaphoreType.DMA((SLOTS + 2,)),
            pltpu.SemaphoreType.DMA((7, NZ)),
            pltpu.SemaphoreType.DMA((7, NZ)),
            pltpu.SemaphoreType.DMA((10, NY)),
            pltpu.SemaphoreType.DMA((10, NY)),
            pltpu.SemaphoreType.DMA,
            pltpu.VMEM((TOK, 1024), bf16),
            pltpu.VMEM((TOK, 128), bf16),
            pltpu.VMEM((4, 128), jnp.int32),
            pltpu.SemaphoreType.DMA((4,)),
        ],
        compiler_params=pltpu.CompilerParams(
            collective_id=0, has_side_effects=True, vmem_limit_bytes=56 * 2**20
        ),
        cost_estimate=pl.CostEstimate(
            flops=14 * 10**9, bytes_accessed=10 * 2**20, transcendentals=19 * 10**6
        ),
    )(queries, key_states, value_states, doc_ids.reshape(4, 128), out_weight)
    return (one.astype(f32) + two.astype(f32)).astype(bf16)


def solution(mesh):
    return jax.shard_map(
        on_device,
        mesh=mesh,
        in_specs=(P("ctx", "head"), P("ctx", "head"), P("ctx", "head"), P("ctx"), P("head", None)),
        out_specs=P(("ctx", "head"), None),
        check_vma=False,
    )
```

```python
import jax
import jax.numpy as jnp
from jax import lax
from jax.experimental import pallas as pl
from jax.experimental.pallas import tpu as pltpu
from jax.sharding import PartitionSpec as P

DH = 128
TOK = 512
VROWS = 144
IDS = 2 * TOK
BLOCK = IDS + 16
SLOTS = 9
RELAY_X, RELAY_Y = 9, 10
UNITS = 16
D_OUT = 4096
PCOLS = 512
NY, NZ = 4, 4
EXP_SCALE = DH**-0.5 * 1.4426950408889634
FAR = -1e30
MESH = pl.DeviceIdType.MESH
NT = (((1,), (1,)), ((), ()))
bf16 = jnp.bfloat16
f32 = jnp.float32


def kernel(
    q_hbm, k_hbm, v_hbm, ids_hbm, w_hbm, one_ref, two_ref,
    kv, kf, qx, s0, s1, mx0, mx1, top, acc, att, w,
    part_z, a_z, b_z, up_z, down_z, mate_out, mate_in,
    part_y, met_y, sum_y, far_y, near_y,
    kv_send, kv_recv, z_send, z_recv, y_send, y_recv, w_sem, q_ref, v_ref, ids_ref, in_sem,
):
    c = lax.axis_index("ctx")
    h = lax.axis_index("head")
    x = c // 4
    y_hi = (c // 2) % 2
    core = c % 2
    y_lo = h // 4
    z = h % 4

    def at_x(step):
        return (((x + step) % 4) * 4 + y_hi * 2 + core, h)

    def at_z(step):
        return (c, y_lo * 4 + (z + step) % 4)

    x_next, x_prev, x_far = at_x(1), at_x(3), at_x(2)
    y_pair = (x * 4 + (1 - y_hi) * 2 + core, h)
    sibling = (x * 4 + y_hi * 2 + 1 - core, h)
    z_next, z_prev = at_z(1), at_z(3)
    y_mate = (c, (1 - y_lo) * 4 + z)

    ids_copy = pltpu.make_async_copy(ids_hbm, ids_ref, in_sem.at[0])
    ids_copy.start()
    v_copy = pltpu.make_async_copy(v_hbm, v_ref, in_sem.at[1])
    v_copy.start()
    k_copy = pltpu.make_async_copy(k_hbm, kv.at[0, pl.ds(0, TOK)], in_sem.at[2])
    k_copy.start()
    q_copy = pltpu.make_async_copy(q_hbm, q_ref, in_sem.at[3])
    q_copy.start()
    w_copy = pltpu.make_async_copy(w_hbm, w, w_sem)
    w_copy.start()

    barrier = pltpu.get_barrier_semaphore()
    for peer in (x_next, x_prev, x_far, y_pair, sibling, z_next, z_prev, y_mate):
        pl.semaphore_signal(barrier, inc=1, device_id=peer, device_id_type=MESH)

    ids_copy.wait()
    kv[0, IDS:BLOCK, :] = jnp.concatenate(
        [ids_ref[...].astype(f32), jnp.zeros((12, 128), f32)], axis=0
    ).astype(bf16)
    v_copy.wait()
    for r in range(4):
        kv[0, TOK + r * 128 : TOK + (r + 1) * 128, :] = (
            v_ref[r * 128 : (r + 1) * 128, :].astype(f32).T.astype(bf16)
        )
    k_copy.wait()

    pl.semaphore_wait(barrier, 8)

    def kv_copy(src, dst, send, peer, half):
        rows = (pl.ds(0, TOK), pl.ds(TOK, BLOCK - TOK))[half]
        return pltpu.make_async_remote_copy(
            src_ref=kv.at[src, rows],
            dst_ref=kv.at[dst, rows],
            send_sem=kv_send.at[send, half],
            recv_sem=kv_recv.at[dst, half],
            device_id=peer,
            device_id_type=MESH,
        )

    def arrived(slot, half=None):
        for part_of in (0, 1) if half is None else (half,):
            kv_copy(slot, slot, 0, sibling, part_of).wait_recv()

    @pl.when(y_hi == 0)
    def _():
        for half in range(2):
            kv_copy(0, 4, 0, x_next, half).start()
            kv_copy(0, 2, 1, y_pair, half).start()
            kv_copy(0, RELAY_X, 2, x_prev, half).start()

    @pl.when(y_hi == 1)
    def _():
        for half in range(2):
            kv_copy(0, 8, 0, x_far, half).start()
            kv_copy(0, RELAY_Y, 1, y_pair, half).start()

    def share(slot, half):
        @pl.when(core == 0)
        def _():
            if slot < 8:
                kv_copy(slot, slot + 1, 6 + slot // 2, sibling, half).start()

        @pl.when(core == 1)
        def _():
            if slot > 0:
                kv_copy(slot, slot - 1, 5 + slot // 2, sibling, half).start()

    share(0, 0)
    share(0, 1)

    lane = lax.broadcasted_iota(jnp.int32, (128, 128), 1).astype(f32)

    def id_columns(slot, r):
        row = kv[slot, IDS:BLOCK, :].astype(f32)[r : r + 1, :]
        return jnp.broadcast_to(row, (128, 128)).T

    def key_marks(slot):
        shift = jnp.where(c >= slot, 0.0, 1000.0)
        for r in range(4):
            kf[slot, r * 128 : (r + 1) * 128, :] = jnp.where(
                id_columns(slot, r) + shift == lane, 0.0, FAR
            ).astype(bf16)

    order = ((2, 2), (3, 1), (1, 3), (0, 0))
    firsts = [(((z + low) % 4) * 64, ((z + high) % 4) * 64 + 256) for low, high in order]

    q_copy.wait()

    for r in range(4):
        kf[0, r * 128 : (r + 1) * 128, :] = jnp.where(id_columns(0, r) == lane, 1.0, 0.0).astype(bf16)
    for t in range(4):
        for half in range(2):
            rows = pl.ds(pl.multiple_of(firsts[t][half], 64), 64)
            marks = kf[0, rows, :]
            for g in range(4):
                for j in range(2):
                    place = j * 128 + half * 64
                    head = 2 * g + j
                    qx[t * 4 + g, place : place + 64, 0:128] = q_ref[rows, head * 128 : (head + 1) * 128]
                    qx[t * 4 + g, place : place + 64, 128:256] = marks
    key_marks(0)

    ones = jnp.ones((VROWS - 128, TOK), bf16)
    key_index = lax.broadcasted_iota(jnp.int32, (TOK, 256), 0)
    lane_q = lax.broadcasted_iota(jnp.int32, (1, 256), 1) % 128

    def score(unit, slot, i, s_ref, diagonal):
        keys = jnp.concatenate([kv[slot, 0:TOK, :], kf[slot]], axis=1)
        s = lax.dot_general(keys, qx[unit], NT, preferred_element_type=f32)
        if diagonal:
            t = unit // 4
            low = jnp.where(t == 0, 2, jnp.where(t == 1, 3, jnp.where(t == 2, 1, 0)))
            high = jnp.where(t == 0, 2, jnp.where(t == 1, 1, jnp.where(t == 2, 3, 0)))
            low_first = ((z + low) % 4) * 64
            high_first = ((z + high) % 4) * 64 + 192
            q_index = lane_q + jnp.where(lane_q < 64, low_first, high_first)
            s = jnp.where(key_index <= q_index, s, FAR)
        s_ref[i * TOK : (i + 1) * TOK, :] = s
        return jnp.max(s.reshape(TOK // 8, 8, 256), axis=0)

    def weigh(slot, i, s_ref, new_top):
        values = jnp.concatenate(
            [kv[slot, TOK + r * 128 : TOK + (r + 1) * 128, :] for r in range(4)], axis=1
        )
        values = jnp.concatenate([values, ones], axis=0)
        probs = jnp.exp2((s_ref[i * TOK : (i + 1) * TOK, :] - new_top) * EXP_SCALE).astype(bf16)
        return jnp.dot(values, probs, preferred_element_type=f32)

    def stage(ahead, now, slots, into, held, diagonal):
        if now is not None:
            new_top = jnp.max(held[1][...], axis=0, keepdims=True)
            if not diagonal:
                old_top = top[now]
                new_top = jnp.maximum(old_top, new_top)
        highest, add = None, None
        for i, slot in enumerate(slots):
            if ahead is not None:
                here = score(ahead, slot, i, into[0], diagonal)
                highest = here if highest is None else jnp.maximum(highest, here)
            if now is not None:
                here = weigh(slot, i, held[0], new_top)
                add = here if add is None else add + here
        if ahead is not None:
            into[1][...] = highest
        if now is not None:
            if diagonal:
                acc[now] = add
            else:
                acc[now] = acc[now] * jnp.exp2((old_top - new_top) * EXP_SCALE) + add
            top[now] = new_top

    pair = ((s0, mx0), (s1, mx1))

    def run(first, count, slots, diagonal=False):
        stage(first, None, slots, pair[0], None, diagonal)

        def body(i, carry):
            for e in range(4):
                now = first + 4 * i + e
                ahead = now + 1
                if e == 3:
                    ahead = None if count == 4 else jnp.minimum(ahead, first + count - 1)
                stage(ahead, now, slots, pair[(e + 1) % 2], pair[e % 2], diagonal)
            return carry

        if count == 4:
            body(0, 0)
        else:
            lax.fori_loop(0, count // 4, body, 0)

    run(0, UNITS, (0,), True)

    @pl.when(y_hi == 0)
    def _():
        for half in range(2):
            arrived(4, half)
            kv_copy(4, 6, 3, y_pair, half).start()
            share(4, half)
            arrived(RELAY_X, half)
            kv_copy(RELAY_X, 8, 4, x_prev, half).start()
            arrived(RELAY_Y, half)
            kv_copy(RELAY_Y, 2, 5, x_next, half).start()

    @pl.when(y_hi == 1)
    def _():
        for half in range(2):
            arrived(8, half)
            kv_copy(8, 6, 3, y_pair, half).start()
            kv_copy(0, 4, 2, x_next, half).start()
            share(8, half)
            arrived(2, half)
            share(2, half)

    early = (4 + 4 * y_hi, 2 * y_hi + (1 - y_hi) * (3 + 2 * core))
    late = (
        2 - y_hi, 6 - 2 * y_hi, 8 - 2 * y_hi, 1 + 2 * y_hi, 5 - 2 * core * (1 - y_hi), 7,
    )
    key_marks(early[0])

    @pl.when(y_hi == 0)
    def _():
        @pl.when(core == 0)
        def _():
            arrived(3)

        @pl.when(core == 1)
        def _():
            arrived(5)

    key_marks(early[1])
    run(0, UNITS, early)

    @pl.when(y_hi == 0)
    def _():
        for half in range(2):
            for slot in (2, 6, 8):
                arrived(slot, half)
                share(slot, half)

    @pl.when(y_hi == 1)
    def _():
        for half in range(2):
            for slot in (4, 6):
                arrived(slot, half)
                share(slot, half)
        arrived(1)

    for slot in late[:3]:
        key_marks(slot)

    def arrive_last():
        @pl.when(y_hi == 0)
        def _():
            arrived(1)

            @pl.when(core == 0)
            def _():
                arrived(5)

            @pl.when(core == 1)
            def _():
                arrived(3)

        @pl.when(y_hi == 1)
        def _():
            arrived(3)
            arrived(5)

        arrived(7)
        for slot in late[3:]:
            key_marks(slot)

    w_copy.wait()

    def z_copy(kind, n):
        low, high = pl.ds(0, 64), pl.ds(64, 64)
        src, dst, peer = (
            (part_z.at[0, n, low], a_z.at[n], z_next),
            (part_z.at[0, n, high], b_z.at[n], z_prev),
            (part_z.at[1, n, high], up_z.at[n, high], z_next),
            (part_z.at[2, n, low], up_z.at[n, low], z_next),
            (part_z.at[1, n, low], down_z.at[n, low], z_prev),
            (part_z.at[2, n, high], down_z.at[n, high], z_prev),
            (mate_out.at[n], mate_in.at[n], y_mate),
        )[kind]
        return pltpu.make_async_remote_copy(
            src_ref=src, dst_ref=dst, send_sem=z_send.at[kind, n], recv_sem=z_recv.at[kind, n],
            device_id=peer, device_id_type=MESH,
        )

    mine = pl.ds(pl.multiple_of(y_lo * 64, 64), 64)
    theirs = pl.ds(pl.multiple_of(64 - y_lo * 64, 64), 64)

    def way(t):
        return (t + y_lo) % 2

    def half_of(t, with_far):
        first = 32 * way(t) if with_far else 32 - 32 * way(t)
        return pl.ds(pl.multiple_of(first, 32), 32)

    def y_copy(kind, n):
        place = kind
        if kind < 4:
            src, dst, peer = part_y.at[kind, n, theirs], met_y.at[kind, n], y_mate
        elif kind < 6:
            src = sum_y.at[0, n, pl.ds(32 * (kind - 4), 32)]
            dst, peer = far_y.at[kind - 4, n], (z_next, z_prev)[kind - 4]
        else:
            t, with_far = kind // 2 - 2, kind % 2
            rows = half_of(t, with_far)
            src, dst, peer = sum_y.at[t, n, rows], near_y.at[way(t), n, rows], at_z(1 + 2 * way(t))
            place = 6 + 2 * way(t) + with_far
        return pltpu.make_async_remote_copy(
            src_ref=src, dst_ref=dst, send_sem=y_send.at[kind, n], recv_sem=y_recv.at[place, n],
            device_id=peer, device_id_type=MESH,
        )

    def meet(t):
        for n in range(NY):
            y_copy(t, n).wait_recv()
            sum_y[t, n] = (part_y[t, n, mine].astype(f32) + met_y[t, n].astype(f32)).astype(bf16)
            for kind in ((4, 5), (6,), (8,))[t]:
                y_copy(kind, n).start()

    def add_far_z():
        for n in range(NZ):
            z_copy(0, n).wait_recv()
            part_z[2, n, 0:64] = (part_z[2, n, 0:64].astype(f32) + a_z[n].astype(f32)).astype(bf16)
            z_copy(3, n).start()
            z_copy(1, n).wait_recv()
            part_z[2, n, 64:128] = (part_z[2, n, 64:128].astype(f32) + b_z[n].astype(f32)).astype(bf16)
            z_copy(5, n).start()

    def add_far_y():
        for n in range(NY):
            y_copy(4, n).wait_recv()
            y_copy(5, n).wait_recv()
            for t in (1, 2):
                rows = half_of(t, 1)
                sum_y[t, n, rows] = (
                    sum_y[t, n, rows].astype(f32) + far_y[way(t), n].astype(f32)
                ).astype(bf16)
                y_copy(5 + 2 * t, n).start()

    for t in range(4):
        if t == 0:
            run(0, 4, late[:3])
            arrive_last()
            run(0, 4, late[3:])
        else:
            run(t * 4, 4, late)
        for g in range(4):
            state = acc[t * 4 + g]
            rows = state[0:128] / state[128:129]
            for j in range(2):
                head = 2 * g + j
                att[:, head * 128 : (head + 1) * 128] = rows[:, j * 128 : (j + 1) * 128].T.astype(bf16)

        for n in range(NY + NZ):
            piece = jnp.dot(
                att[...], w[:, n * PCOLS : (n + 1) * PCOLS], preferred_element_type=f32
            ).astype(bf16)
            if n < NY:
                part_y[t, n] = piece
            else:
                part_z[t, n - NY] = piece
            if n == NY - 1:
                for i in range(NY):
                    y_copy(t, i).start()
            if n == NY + 1 or n == NY + 3:
                for i in (n - NY - 1, n - NY):
                    for kind in ((0, 1), (2, 4), (), ())[t]:
                        z_copy(kind, i).start()
        if t > 0:
            meet(t - 1)
        if t == 2:
            add_far_z()

    add_far_y()

    def total_z(n, rows):
        return (
            part_z[3, n, rows].astype(f32) + up_z[n, rows].astype(f32) + down_z[n, rows].astype(f32)
        )

    for n in range(NZ):
        for kind in (2, 3, 4, 5):
            z_copy(kind, n).wait_recv()
        mate_out[n] = total_z(n, theirs).astype(bf16)
        z_copy(6, n).start()

    for n in range(NZ):
        one_ref[:, (NY + n) * PCOLS : (NY + n + 1) * PCOLS] = total_z(n, mine).astype(bf16)

    for n in range(NY):
        y_copy(3, n).wait_recv()
        one_ref[:, n * PCOLS : (n + 1) * PCOLS] = (
            part_y[3, n, mine].astype(f32) + met_y[3, n].astype(f32)
        ).astype(bf16)

    for n in range(NY):
        for kind in (6, 7, 8, 9):
            y_copy(kind, n).wait_recv()
        two_ref[:, n * PCOLS : (n + 1) * PCOLS] = (
            near_y[0, n].astype(f32) + near_y[1, n].astype(f32)
        ).astype(bf16)

    for n in range(NZ):
        z_copy(6, n).wait_recv()
        two_ref[:, (NY + n) * PCOLS : (NY + n + 1) * PCOLS] = mate_in[n]

    for half in range(2):
        for send in (0, 1, 2, 3, 6, 7, 8, 9):
            kv_copy(0, 0, send, sibling, half).wait_send()

    @pl.when(y_hi == 0)
    def _():
        for half in range(2):
            for send in (4, 5):
                kv_copy(0, 0, send, sibling, half).wait_send()

    for n in range(NZ):
        for kind in range(7):
            z_copy(kind, n).wait_send()
    for n in range(NY):
        for kind in range(10):
            y_copy(kind, n).wait_send()


def on_device(queries, key_states, value_states, doc_ids, out_weight):
    vmem = pl.BlockSpec(memory_space=pltpu.VMEM)
    one, two = pl.pallas_call(
        kernel,
        name="attend_project",
        out_shape=[jax.ShapeDtypeStruct((64, D_OUT), bf16)] * 2,
        in_specs=[pl.BlockSpec(memory_space=pl.ANY)] * 5,
        out_specs=[vmem, vmem],
        scratch_shapes=[
            pltpu.VMEM((SLOTS + 2, BLOCK, 128), bf16),
            pltpu.VMEM((SLOTS, TOK, 128), bf16),
            pltpu.VMEM((UNITS, 256, 256), bf16),
            pltpu.VMEM((6 * TOK, 256), f32),
            pltpu.VMEM((6 * TOK, 256), f32),
            pltpu.VMEM((8, 256), f32),
            pltpu.VMEM((8, 256), f32),
            pltpu.VMEM((UNITS, 1, 256), f32),
            pltpu.VMEM((UNITS, VROWS, 256), f32),
            pltpu.VMEM((128, 1024), bf16),
            pltpu.VMEM((1024, D_OUT), bf16),
            pltpu.VMEM((4, NZ, 128, PCOLS), bf16),
            pltpu.VMEM((NZ, 64, PCOLS), bf16),
            pltpu.VMEM((NZ, 64, PCOLS), bf16),
            pltpu.VMEM((NZ, 128, PCOLS), bf16),
            pltpu.VMEM((NZ, 128, PCOLS), bf16),
            pltpu.VMEM((NZ, 64, PCOLS), bf16),
            pltpu.VMEM((NZ, 64, PCOLS), bf16),
            pltpu.VMEM((4, NY, 128, PCOLS), bf16),
            pltpu.VMEM((4, NY, 64, PCOLS), bf16),
            pltpu.VMEM((3, NY, 64, PCOLS), bf16),
            pltpu.VMEM((2, NY, 32, PCOLS), bf16),
            pltpu.VMEM((2, NY, 64, PCOLS), bf16),
            pltpu.SemaphoreType.DMA((10, 2)),
            pltpu.SemaphoreType.DMA((SLOTS + 2, 2)),
            pltpu.SemaphoreType.DMA((7, NZ)),
            pltpu.SemaphoreType.DMA((7, NZ)),
            pltpu.SemaphoreType.DMA((10, NY)),
            pltpu.SemaphoreType.DMA((10, NY)),
            pltpu.SemaphoreType.DMA,
            pltpu.VMEM((TOK, 1024), bf16),
            pltpu.VMEM((TOK, 128), bf16),
            pltpu.VMEM((4, 128), jnp.int32),
            pltpu.SemaphoreType.DMA((4,)),
        ],
        compiler_params=pltpu.CompilerParams(
            collective_id=0, has_side_effects=True, vmem_limit_bytes=52 * 2**20
        ),
        cost_estimate=pl.CostEstimate(
            flops=14 * 10**9, bytes_accessed=10 * 2**20, transcendentals=19 * 10**6
        ),
    )(queries, key_states, value_states, doc_ids.reshape(4, 128), out_weight)
    return (one.astype(f32) + two.astype(f32)).astype(bf16)


def solution(mesh):
    return jax.shard_map(
        on_device,
        mesh=mesh,
        in_specs=(P("ctx", "head"), P("ctx", "head"), P("ctx", "head"), P("ctx"), P("head", None)),
        out_specs=P(("ctx", "head"), None),
        check_vma=False,
    )
```

```python
import jax
import jax.numpy as jnp
from jax import lax
from jax.experimental import pallas as pl
from jax.experimental.pallas import tpu as pltpu
from jax.sharding import PartitionSpec as P

DH = 128
TOK = 512
VROWS = 144
IDS = 2 * TOK
BLOCK = IDS + 16
SLOTS = 9
RELAY_X, RELAY_Y = 9, 10
UNITS = 16
D_OUT = 4096
PCOLS = 512
NY, NZ = 4, 4
EXP_SCALE = DH**-0.5 * 1.4426950408889634
FAR = -1e30
MESH = pl.DeviceIdType.MESH
NT = (((1,), (1,)), ((), ()))
bf16 = jnp.bfloat16
f32 = jnp.float32


def kernel(
    q_hbm, k_hbm, v_hbm, ids_hbm, w_hbm, one_ref, two_ref,
    kv, kf, qx, s0, s1, mx0, mx1, top, acc, att, w,
    part_z, a_z, b_z, up_z, down_z, mate_out, mate_in,
    part_y, met_y, sum_y, far_y, near_y,
    kv_send, kv_recv, z_send, z_recv, y_send, y_recv, w_sem, q_ref, v_ref, ids_ref, in_sem,
):
    c = lax.axis_index("ctx")
    h = lax.axis_index("head")
    x = c // 4
    y_hi = (c // 2) % 2
    core = c % 2
    y_lo = h // 4
    z = h % 4

    def at_x(step):
        return (((x + step) % 4) * 4 + y_hi * 2 + core, h)

    def at_z(step):
        return (c, y_lo * 4 + (z + step) % 4)

    x_next, x_prev, x_far = at_x(1), at_x(3), at_x(2)
    y_pair = (x * 4 + (1 - y_hi) * 2 + core, h)
    sibling = (x * 4 + y_hi * 2 + 1 - core, h)
    z_next, z_prev = at_z(1), at_z(3)
    y_mate = (c, (1 - y_lo) * 4 + z)

    ids_copy = pltpu.make_async_copy(ids_hbm, ids_ref, in_sem.at[0])
    ids_copy.start()
    v_copy = pltpu.make_async_copy(v_hbm, v_ref, in_sem.at[1])
    v_copy.start()
    k_copy = pltpu.make_async_copy(k_hbm, kv.at[0, pl.ds(0, TOK)], in_sem.at[2])
    k_copy.start()
    q_copy = pltpu.make_async_copy(q_hbm, q_ref, in_sem.at[3])
    q_copy.start()
    w_copy = pltpu.make_async_copy(w_hbm, w, w_sem)
    w_copy.start()

    barrier = pltpu.get_barrier_semaphore()
    for peer in (x_next, x_prev, x_far, y_pair, sibling, z_next, z_prev, y_mate):
        pl.semaphore_signal(barrier, inc=1, device_id=peer, device_id_type=MESH)

    ids_copy.wait()
    kv[0, IDS:BLOCK, :] = jnp.concatenate(
        [ids_ref[...].astype(f32), jnp.zeros((12, 128), f32)], axis=0
    ).astype(bf16)
    v_copy.wait()
    for r in range(4):
        kv[0, TOK + r * 128 : TOK + (r + 1) * 128, :] = (
            v_ref[r * 128 : (r + 1) * 128, :].astype(f32).T.astype(bf16)
        )
    k_copy.wait()

    pl.semaphore_wait(barrier, 8)

    def kv_copy(src, dst, send, peer):
        return pltpu.make_async_remote_copy(
            src_ref=kv.at[src],
            dst_ref=kv.at[dst],
            send_sem=kv_send.at[send],
            recv_sem=kv_recv.at[dst],
            device_id=peer,
            device_id_type=MESH,
        )

    def arrived(slot):
        kv_copy(slot, slot, 0, sibling).wait_recv()

    @pl.when(y_hi == 0)
    def _():
        kv_copy(0, 4, 0, x_next).start()
        kv_copy(0, 2, 1, y_pair).start()
        kv_copy(0, RELAY_X, 2, x_prev).start()

    @pl.when(y_hi == 1)
    def _():
        kv_copy(0, 8, 0, x_far).start()
        kv_copy(0, RELAY_Y, 1, y_pair).start()

    def share(slot):
        @pl.when(core == 0)
        def _():
            if slot < 8:
                kv_copy(slot, slot + 1, 6 + slot // 2, sibling).start()

        @pl.when(core == 1)
        def _():
            if slot > 0:
                kv_copy(slot, slot - 1, 5 + slot // 2, sibling).start()

    share(0)

    lane = lax.broadcasted_iota(jnp.int32, (128, 128), 1).astype(f32)

    def id_columns(slot, r):
        row = kv[slot, IDS:BLOCK, :].astype(f32)[r : r + 1, :]
        return jnp.broadcast_to(row, (128, 128)).T

    def key_marks(slot):
        shift = jnp.where(c >= slot, 0.0, 1000.0)
        for r in range(4):
            kf[slot, r * 128 : (r + 1) * 128, :] = jnp.where(
                id_columns(slot, r) + shift == lane, 0.0, FAR
            ).astype(bf16)

    order = ((2, 2), (3, 1), (1, 3), (0, 0))
    firsts = [(((z + low) % 4) * 64, ((z + high) % 4) * 64 + 256) for low, high in order]

    q_copy.wait()

    for r in range(4):
        kf[0, r * 128 : (r + 1) * 128, :] = jnp.where(id_columns(0, r) == lane, 1.0, 0.0).astype(bf16)
    for t in range(4):
        for half in range(2):
            rows = pl.ds(pl.multiple_of(firsts[t][half], 64), 64)
            marks = kf[0, rows, :]
            for g in range(4):
                for j in range(2):
                    place = j * 128 + half * 64
                    head = 2 * g + j
                    qx[t * 4 + g, place : place + 64, 0:128] = q_ref[rows, head * 128 : (head + 1) * 128]
                    qx[t * 4 + g, place : place + 64, 128:256] = marks
    key_marks(0)

    ones = jnp.ones((VROWS - 128, TOK), bf16)
    key_index = lax.broadcasted_iota(jnp.int32, (TOK, 256), 0)
    lane_q = lax.broadcasted_iota(jnp.int32, (1, 256), 1) % 128

    def score(unit, slot, i, s_ref, diagonal):
        keys = jnp.concatenate([kv[slot, 0:TOK, :], kf[slot]], axis=1)
        s = lax.dot_general(keys, qx[unit], NT, preferred_element_type=f32)
        if diagonal:
            t = unit // 4
            low = jnp.where(t == 0, 2, jnp.where(t == 1, 3, jnp.where(t == 2, 1, 0)))
            high = jnp.where(t == 0, 2, jnp.where(t == 1, 1, jnp.where(t == 2, 3, 0)))
            low_first = ((z + low) % 4) * 64
            high_first = ((z + high) % 4) * 64 + 192
            q_index = lane_q + jnp.where(lane_q < 64, low_first, high_first)
            s = jnp.where(key_index <= q_index, s, FAR)
        s_ref[i * TOK : (i + 1) * TOK, :] = s
        return jnp.max(s.reshape(TOK // 8, 8, 256), axis=0)

    def weigh(slot, i, s_ref, new_top):
        values = jnp.concatenate(
            [kv[slot, TOK + r * 128 : TOK + (r + 1) * 128, :] for r in range(4)], axis=1
        )
        values = jnp.concatenate([values, ones], axis=0)
        probs = jnp.exp2((s_ref[i * TOK : (i + 1) * TOK, :] - new_top) * EXP_SCALE).astype(bf16)
        return jnp.dot(values, probs, preferred_element_type=f32)

    def stage(ahead, now, slots, into, held, diagonal):
        if now is not None:
            new_top = jnp.max(held[1][...], axis=0, keepdims=True)
            if not diagonal:
                old_top = top[now]
                new_top = jnp.maximum(old_top, new_top)
        highest, add = None, None
        for i, slot in enumerate(slots):
            if ahead is not None:
                here = score(ahead, slot, i, into[0], diagonal)
                highest = here if highest is None else jnp.maximum(highest, here)
            if now is not None:
                here = weigh(slot, i, held[0], new_top)
                add = here if add is None else add + here
        if ahead is not None:
            into[1][...] = highest
        if now is not None:
            if diagonal:
                acc[now] = add
            else:
                acc[now] = acc[now] * jnp.exp2((old_top - new_top) * EXP_SCALE) + add
            top[now] = new_top

    pair = ((s0, mx0), (s1, mx1))

    def run(first, count, slots, diagonal=False):
        stage(first, None, slots, pair[0], None, diagonal)

        def body(i, carry):
            for e in range(4):
                now = first + 4 * i + e
                ahead = now + 1
                if e == 3:
                    ahead = None if count == 4 else jnp.minimum(ahead, first + count - 1)
                stage(ahead, now, slots, pair[(e + 1) % 2], pair[e % 2], diagonal)
            return carry

        if count == 4:
            body(0, 0)
        else:
            lax.fori_loop(0, count // 4, body, 0)

    run(0, UNITS, (0,), True)

    @pl.when(y_hi == 0)
    def _():
        arrived(4)
        kv_copy(4, 6, 3, y_pair).start()
        share(4)
        arrived(RELAY_X)
        kv_copy(RELAY_X, 8, 4, x_prev).start()
        arrived(RELAY_Y)
        kv_copy(RELAY_Y, 2, 5, x_next).start()

    @pl.when(y_hi == 1)
    def _():
        arrived(8)
        kv_copy(8, 6, 3, y_pair).start()
        kv_copy(0, 4, 2, x_next).start()
        share(8)
        arrived(2)
        share(2)

    early = (4 + 4 * y_hi, 2 * y_hi + (1 - y_hi) * (3 + 2 * core))
    late = (
        2 - y_hi, 6 - 2 * y_hi, 8 - 2 * y_hi, 1 + 2 * y_hi, 5 - 2 * core * (1 - y_hi), 7,
    )
    key_marks(early[0])

    @pl.when(y_hi == 0)
    def _():
        @pl.when(core == 0)
        def _():
            arrived(3)

        @pl.when(core == 1)
        def _():
            arrived(5)

    key_marks(early[1])
    run(0, UNITS, early)

    @pl.when(y_hi == 0)
    def _():
        arrived(2)
        share(2)
        arrived(6)
        share(6)
        arrived(8)
        share(8)

    @pl.when(y_hi == 1)
    def _():
        arrived(4)
        share(4)
        arrived(6)
        share(6)
        arrived(1)

    for slot in late[:3]:
        key_marks(slot)

    def arrive_last():
        @pl.when(y_hi == 0)
        def _():
            arrived(1)

            @pl.when(core == 0)
            def _():
                arrived(5)

            @pl.when(core == 1)
            def _():
                arrived(3)

        @pl.when(y_hi == 1)
        def _():
            arrived(3)
            arrived(5)

        arrived(7)
        for slot in late[3:]:
            key_marks(slot)

    w_copy.wait()

    def z_copy(kind, n):
        low, high = pl.ds(0, 64), pl.ds(64, 64)
        src, dst, peer = (
            (part_z.at[0, n, low], a_z.at[n], z_next),
            (part_z.at[0, n, high], b_z.at[n], z_prev),
            (part_z.at[1, n, high], up_z.at[n, high], z_next),
            (part_z.at[2, n, low], up_z.at[n, low], z_next),
            (part_z.at[1, n, low], down_z.at[n, low], z_prev),
            (part_z.at[2, n, high], down_z.at[n, high], z_prev),
            (mate_out.at[n], mate_in.at[n], y_mate),
        )[kind]
        return pltpu.make_async_remote_copy(
            src_ref=src, dst_ref=dst, send_sem=z_send.at[kind, n], recv_sem=z_recv.at[kind, n],
            device_id=peer, device_id_type=MESH,
        )

    mine = pl.ds(pl.multiple_of(y_lo * 64, 64), 64)
    theirs = pl.ds(pl.multiple_of(64 - y_lo * 64, 64), 64)

    def way(t):
        return (t + y_lo) % 2

    def half_of(t, with_far):
        first = 32 * way(t) if with_far else 32 - 32 * way(t)
        return pl.ds(pl.multiple_of(first, 32), 32)

    def y_copy(kind, n):
        place = kind
        if kind < 4:
            src, dst, peer = part_y.at[kind, n, theirs], met_y.at[kind, n], y_mate
        elif kind < 6:
            src = sum_y.at[0, n, pl.ds(32 * (kind - 4), 32)]
            dst, peer = far_y.at[kind - 4, n], (z_next, z_prev)[kind - 4]
        else:
            t, with_far = kind // 2 - 2, kind % 2
            rows = half_of(t, with_far)
            src, dst, peer = sum_y.at[t, n, rows], near_y.at[way(t), n, rows], at_z(1 + 2 * way(t))
            place = 6 + 2 * way(t) + with_far
        return pltpu.make_async_remote_copy(
            src_ref=src, dst_ref=dst, send_sem=y_send.at[kind, n], recv_sem=y_recv.at[place, n],
            device_id=peer, device_id_type=MESH,
        )

    def meet(t):
        for n in range(NY):
            y_copy(t, n).wait_recv()
            sum_y[t, n] = (part_y[t, n, mine].astype(f32) + met_y[t, n].astype(f32)).astype(bf16)
            for kind in ((4, 5), (6,), (8,))[t]:
                y_copy(kind, n).start()

    def add_far_z():
        for n in range(NZ):
            z_copy(0, n).wait_recv()
            part_z[2, n, 0:64] = (part_z[2, n, 0:64].astype(f32) + a_z[n].astype(f32)).astype(bf16)
            z_copy(3, n).start()
            z_copy(1, n).wait_recv()
            part_z[2, n, 64:128] = (part_z[2, n, 64:128].astype(f32) + b_z[n].astype(f32)).astype(bf16)
            z_copy(5, n).start()

    def add_far_y():
        for n in range(NY):
            y_copy(4, n).wait_recv()
            y_copy(5, n).wait_recv()
            for t in (1, 2):
                rows = half_of(t, 1)
                sum_y[t, n, rows] = (
                    sum_y[t, n, rows].astype(f32) + far_y[way(t), n].astype(f32)
                ).astype(bf16)
                y_copy(5 + 2 * t, n).start()

    for t in range(4):
        if t == 0:
            run(0, 4, late[:3])
            arrive_last()
            run(0, 4, late[3:])
        else:
            run(t * 4, 4, late)
        for g in range(4):
            state = acc[t * 4 + g]
            rows = state[0:128] / state[128:129]
            for j in range(2):
                head = 2 * g + j
                att[:, head * 128 : (head + 1) * 128] = rows[:, j * 128 : (j + 1) * 128].T.astype(bf16)

        for n in range(NY + NZ):
            piece = jnp.dot(
                att[...], w[:, n * PCOLS : (n + 1) * PCOLS], preferred_element_type=f32
            ).astype(bf16)
            if n < NY:
                part_y[t, n] = piece
            else:
                part_z[t, n - NY] = piece
            if n == NY - 1:
                for i in range(NY):
                    y_copy(t, i).start()
            if n == NY + 1 or n == NY + 3:
                for i in (n - NY - 1, n - NY):
                    for kind in ((0, 1), (2, 4), (), ())[t]:
                        z_copy(kind, i).start()
        if t > 0:
            meet(t - 1)
        if t == 2:
            add_far_z()

    add_far_y()

    def total_z(n, rows):
        return (
            part_z[3, n, rows].astype(f32) + up_z[n, rows].astype(f32) + down_z[n, rows].astype(f32)
        )

    for n in range(NZ):
        for kind in (2, 3, 4, 5):
            z_copy(kind, n).wait_recv()
        mate_out[n] = total_z(n, theirs).astype(bf16)
        z_copy(6, n).start()

    for n in range(NZ):
        one_ref[:, (NY + n) * PCOLS : (NY + n + 1) * PCOLS] = total_z(n, mine).astype(bf16)

    for n in range(NY):
        y_copy(3, n).wait_recv()
        one_ref[:, n * PCOLS : (n + 1) * PCOLS] = (
            part_y[3, n, mine].astype(f32) + met_y[3, n].astype(f32)
        ).astype(bf16)

    for n in range(NY):
        for kind in (6, 7, 8, 9):
            y_copy(kind, n).wait_recv()
        two_ref[:, n * PCOLS : (n + 1) * PCOLS] = (
            near_y[0, n].astype(f32) + near_y[1, n].astype(f32)
        ).astype(bf16)

    for n in range(NZ):
        z_copy(6, n).wait_recv()
        two_ref[:, (NY + n) * PCOLS : (NY + n + 1) * PCOLS] = mate_in[n]

    for send in (0, 1, 2, 3, 6, 7, 8, 9):
        kv_copy(0, 0, send, sibling).wait_send()

    @pl.when(y_hi == 0)
    def _():
        for send in (4, 5):
            kv_copy(0, 0, send, sibling).wait_send()

    for n in range(NZ):
        for kind in range(7):
            z_copy(kind, n).wait_send()
    for n in range(NY):
        for kind in range(10):
            y_copy(kind, n).wait_send()


def on_device(queries, key_states, value_states, doc_ids, out_weight):
    vmem = pl.BlockSpec(memory_space=pltpu.VMEM)
    in_hbm = [
        pltpu.with_memory_space_constraint(a, pltpu.HBM)
        for a in (queries, key_states, value_states, doc_ids.reshape(4, 128), out_weight)
    ]
    one, two = pl.pallas_call(
        kernel,
        name="attend_project",
        out_shape=[jax.ShapeDtypeStruct((64, D_OUT), bf16)] * 2,
        in_specs=[pl.BlockSpec(memory_space=pl.ANY)] * 5,
        out_specs=[vmem, vmem],
        scratch_shapes=[
            pltpu.VMEM((SLOTS + 2, BLOCK, 128), bf16),
            pltpu.VMEM((SLOTS, TOK, 128), bf16),
            pltpu.VMEM((UNITS, 256, 256), bf16),
            pltpu.VMEM((6 * TOK, 256), f32),
            pltpu.VMEM((6 * TOK, 256), f32),
            pltpu.VMEM((8, 256), f32),
            pltpu.VMEM((8, 256), f32),
            pltpu.VMEM((UNITS, 1, 256), f32),
            pltpu.VMEM((UNITS, VROWS, 256), f32),
            pltpu.VMEM((128, 1024), bf16),
            pltpu.VMEM((1024, D_OUT), bf16),
            pltpu.VMEM((4, NZ, 128, PCOLS), bf16),
            pltpu.VMEM((NZ, 64, PCOLS), bf16),
            pltpu.VMEM((NZ, 64, PCOLS), bf16),
            pltpu.VMEM((NZ, 128, PCOLS), bf16),
            pltpu.VMEM((NZ, 128, PCOLS), bf16),
            pltpu.VMEM((NZ, 64, PCOLS), bf16),
            pltpu.VMEM((NZ, 64, PCOLS), bf16),
            pltpu.VMEM((4, NY, 128, PCOLS), bf16),
            pltpu.VMEM((4, NY, 64, PCOLS), bf16),
            pltpu.VMEM((3, NY, 64, PCOLS), bf16),
            pltpu.VMEM((2, NY, 32, PCOLS), bf16),
            pltpu.VMEM((2, NY, 64, PCOLS), bf16),
            pltpu.SemaphoreType.DMA((10,)),
            pltpu.SemaphoreType.DMA((SLOTS + 2,)),
            pltpu.SemaphoreType.DMA((7, NZ)),
            pltpu.SemaphoreType.DMA((7, NZ)),
            pltpu.SemaphoreType.DMA((10, NY)),
            pltpu.SemaphoreType.DMA((10, NY)),
            pltpu.SemaphoreType.DMA,
            pltpu.VMEM((TOK, 1024), bf16),
            pltpu.VMEM((TOK, 128), bf16),
            pltpu.VMEM((4, 128), jnp.int32),
            pltpu.SemaphoreType.DMA((4,)),
        ],
        compiler_params=pltpu.CompilerParams(
            collective_id=0, has_side_effects=True, vmem_limit_bytes=52 * 2**20
        ),
        cost_estimate=pl.CostEstimate(
            flops=14 * 10**9, bytes_accessed=10 * 2**20, transcendentals=19 * 10**6
        ),
    )(*in_hbm)
    return (one.astype(f32) + two.astype(f32)).astype(bf16)


def solution(mesh):
    return jax.shard_map(
        on_device,
        mesh=mesh,
        in_specs=(P("ctx", "head"), P("ctx", "head"), P("ctx", "head"), P("ctx"), P("head", None)),
        out_specs=P(("ctx", "head"), None),
        check_vma=False,
    )
```

```python
import jax
import jax.numpy as jnp
from jax import lax
from jax.experimental import pallas as pl
from jax.experimental.pallas import tpu as pltpu
from jax.sharding import PartitionSpec as P

DH = 128
TOK = 512
VROWS = 144
IDS = 2 * TOK
BLOCK = IDS + 16
SLOTS = 9
RELAY_X, RELAY_Y = 9, 10
UNITS = 16
D_OUT = 4096
PCOLS = 512
NY, NZ = 4, 4
EXP_SCALE = DH**-0.5 * 1.4426950408889634
FAR = -1e30
MESH = pl.DeviceIdType.MESH
NT = (((1,), (1,)), ((), ()))
bf16 = jnp.bfloat16
f32 = jnp.float32


def kernel(
    q_hbm, k_hbm, v_hbm, ids_hbm, w_hbm, one_ref, two_ref,
    kv, kf, qx, s0, s1, mx0, mx1, top, acc, att, w,
    part_z, a_z, b_z, up_z, down_z, mate_out, mate_in,
    part_y, met_y, sum_y, far_y, near_y,
    kv_send, kv_recv, z_send, z_recv, y_send, y_recv, w_sem, q_ref, v_ref, ids_ref, in_sem,
):
    c = lax.axis_index("ctx")
    h = lax.axis_index("head")
    x = c // 4
    y_hi = (c // 2) % 2
    core = c % 2
    y_lo = h // 4
    z = h % 4

    def at_x(step):
        return (((x + step) % 4) * 4 + y_hi * 2 + core, h)

    def at_z(step):
        return (c, y_lo * 4 + (z + step) % 4)

    x_next, x_prev, x_far = at_x(1), at_x(3), at_x(2)
    y_pair = (x * 4 + (1 - y_hi) * 2 + core, h)
    sibling = (x * 4 + y_hi * 2 + 1 - core, h)
    z_next, z_prev = at_z(1), at_z(3)
    y_mate = (c, (1 - y_lo) * 4 + z)

    ids_copy = pltpu.make_async_copy(ids_hbm, ids_ref, in_sem.at[0])
    ids_copy.start()
    v_copy = pltpu.make_async_copy(v_hbm, v_ref, in_sem.at[1])
    v_copy.start()
    k_copy = pltpu.make_async_copy(k_hbm, kv.at[0, pl.ds(0, TOK)], in_sem.at[2])
    k_copy.start()
    q_copy = pltpu.make_async_copy(q_hbm, q_ref, in_sem.at[3])
    q_copy.start()
    w_copy = pltpu.make_async_copy(w_hbm, w, w_sem)
    w_copy.start()

    barrier = pltpu.get_barrier_semaphore()
    for peer in (x_next, x_prev, x_far, y_pair, sibling, z_next, z_prev, y_mate):
        pl.semaphore_signal(barrier, inc=1, device_id=peer, device_id_type=MESH)

    ids_copy.wait()
    kv[0, IDS:BLOCK, :] = jnp.concatenate(
        [ids_ref[...].astype(f32), jnp.zeros((12, 128), f32)], axis=0
    ).astype(bf16)
    v_copy.wait()
    for r in range(4):
        kv[0, TOK + r * 128 : TOK + (r + 1) * 128, :] = (
            v_ref[r * 128 : (r + 1) * 128, :].astype(f32).T.astype(bf16)
        )
    k_copy.wait()

    pl.semaphore_wait(barrier, 8)

    def kv_copy(src, dst, send, peer):
        return pltpu.make_async_remote_copy(
            src_ref=kv.at[src],
            dst_ref=kv.at[dst],
            send_sem=kv_send.at[send],
            recv_sem=kv_recv.at[dst],
            device_id=peer,
            device_id_type=MESH,
        )

    def arrived(slot):
        kv_copy(slot, slot, 0, sibling).wait_recv()

    @pl.when(y_hi == 0)
    def _():
        kv_copy(0, 4, 0, x_next).start()
        kv_copy(0, 2, 1, y_pair).start()
        kv_copy(0, RELAY_X, 2, x_prev).start()

    @pl.when(y_hi == 1)
    def _():
        kv_copy(0, 8, 0, x_far).start()
        kv_copy(0, RELAY_Y, 1, y_pair).start()

    def share(slot):
        @pl.when(core == 0)
        def _():
            if slot < 8:
                kv_copy(slot, slot + 1, 6 + slot // 2, sibling).start()

        @pl.when(core == 1)
        def _():
            if slot > 0:
                kv_copy(slot, slot - 1, 5 + slot // 2, sibling).start()

    share(0)

    lane = lax.broadcasted_iota(jnp.int32, (128, 128), 1).astype(f32)

    def id_columns(slot, r):
        row = kv[slot, IDS:BLOCK, :].astype(f32)[r : r + 1, :]
        return jnp.broadcast_to(row, (128, 128)).T

    def key_marks(slot):
        shift = jnp.where(c >= slot, 0.0, 1000.0)
        for r in range(4):
            kf[slot, r * 128 : (r + 1) * 128, :] = jnp.where(
                id_columns(slot, r) + shift == lane, 0.0, FAR
            ).astype(bf16)

    order = ((2, 2), (3, 1), (1, 3), (0, 0))
    firsts = [(((z + low) % 4) * 64, ((z + high) % 4) * 64 + 256) for low, high in order]

    q_copy.wait()

    for r in range(4):
        kf[0, r * 128 : (r + 1) * 128, :] = jnp.where(id_columns(0, r) == lane, 1.0, 0.0).astype(bf16)
    for sub in range(2):
        for half in range(2):
            rows = pl.ds(pl.multiple_of(firsts[0][half] + 32 * sub, 32), 32)
            marks = kf[0, rows, :]
            for head in range(8):
                unit, place = 2 * sub + head // 4, head % 4 * 64 + half * 32
                qx[unit, place : place + 32, 0:128] = q_ref[rows, head * 128 : (head + 1) * 128]
                qx[unit, place : place + 32, 128:256] = marks
    for t in range(1, 4):
        for half in range(2):
            rows = pl.ds(pl.multiple_of(firsts[t][half], 64), 64)
            marks = kf[0, rows, :]
            for g in range(4):
                for j in range(2):
                    place = j * 128 + half * 64
                    head = 2 * g + j
                    qx[t * 4 + g, place : place + 64, 0:128] = q_ref[rows, head * 128 : (head + 1) * 128]
                    qx[t * 4 + g, place : place + 64, 128:256] = marks
    key_marks(0)

    ones = jnp.ones((VROWS - 128, TOK), bf16)
    key_index = lax.broadcasted_iota(jnp.int32, (TOK, 256), 0)
    lane_q = lax.broadcasted_iota(jnp.int32, (1, 256), 1) % 128

    def score(unit, slot, i, s_ref, diagonal):
        keys = jnp.concatenate([kv[slot, 0:TOK, :], kf[slot]], axis=1)
        s = lax.dot_general(keys, qx[unit], NT, preferred_element_type=f32)
        if diagonal:
            t = unit // 4
            low = jnp.where(t == 0, 2, jnp.where(t == 1, 3, jnp.where(t == 2, 1, 0)))
            high = jnp.where(t == 0, 2, jnp.where(t == 1, 1, jnp.where(t == 2, 3, 0)))
            low_first = ((z + low) % 4) * 64
            high_first = ((z + high) % 4) * 64 + 192
            q_index = lane_q + jnp.where(lane_q < 64, low_first, high_first)
            lane_0 = lane_q % 64
            q_index_0 = lane_0 + jnp.where(lane_0 < 32, low_first, high_first + 32) + unit // 2 * 32
            q_index = jnp.where(t == 0, q_index_0, q_index)
            s = jnp.where(key_index <= q_index, s, FAR)
        s_ref[i * TOK : (i + 1) * TOK, :] = s
        return jnp.max(s.reshape(TOK // 8, 8, 256), axis=0)

    def weigh(slot, i, s_ref, new_top):
        values = jnp.concatenate(
            [kv[slot, TOK + r * 128 : TOK + (r + 1) * 128, :] for r in range(4)], axis=1
        )
        values = jnp.concatenate([values, ones], axis=0)
        probs = jnp.exp2((s_ref[i * TOK : (i + 1) * TOK, :] - new_top) * EXP_SCALE).astype(bf16)
        return jnp.dot(values, probs, preferred_element_type=f32)

    def stage(ahead, now, slots, into, held, diagonal):
        if now is not None:
            new_top = jnp.max(held[1][...], axis=0, keepdims=True)
            if not diagonal:
                old_top = top[now]
                new_top = jnp.maximum(old_top, new_top)
        highest, add = None, None
        for i, slot in enumerate(slots):
            if ahead is not None:
                here = score(ahead, slot, i, into[0], diagonal)
                highest = here if highest is None else jnp.maximum(highest, here)
            if now is not None:
                here = weigh(slot, i, held[0], new_top)
                add = here if add is None else add + here
        if ahead is not None:
            into[1][...] = highest
        if now is not None:
            if diagonal:
                acc[now] = add
            else:
                acc[now] = acc[now] * jnp.exp2((old_top - new_top) * EXP_SCALE) + add
            top[now] = new_top

    pair = ((s0, mx0), (s1, mx1))

    def run(first, count, slots, diagonal=False):
        stage(first, None, slots, pair[0], None, diagonal)
        steps = min(4, count)

        def body(i, carry):
            for e in range(steps):
                now = first + steps * i + e
                ahead = now + 1
                if e == steps - 1:
                    ahead = None if count == steps else jnp.minimum(ahead, first + count - 1)
                stage(ahead, now, slots, pair[(e + 1) % 2], pair[e % 2], diagonal)
            return carry

        if count == steps:
            body(0, 0)
        else:
            lax.fori_loop(0, count // steps, body, 0)

    run(0, UNITS, (0,), True)

    @pl.when(y_hi == 0)
    def _():
        arrived(4)
        kv_copy(4, 6, 3, y_pair).start()
        share(4)
        arrived(RELAY_X)
        kv_copy(RELAY_X, 8, 4, x_prev).start()
        arrived(RELAY_Y)
        kv_copy(RELAY_Y, 2, 5, x_next).start()

    @pl.when(y_hi == 1)
    def _():
        arrived(8)
        kv_copy(8, 6, 3, y_pair).start()
        kv_copy(0, 4, 2, x_next).start()
        share(8)
        arrived(2)
        share(2)

    early = (4 + 4 * y_hi, 2 * y_hi + (1 - y_hi) * (3 + 2 * core))
    late = (
        2 - y_hi, 6 - 2 * y_hi, 8 - 2 * y_hi, 1 + 2 * y_hi, 5 - 2 * core * (1 - y_hi), 7,
    )
    key_marks(early[0])

    @pl.when(y_hi == 0)
    def _():
        @pl.when(core == 0)
        def _():
            arrived(3)

        @pl.when(core == 1)
        def _():
            arrived(5)

    key_marks(early[1])
    run(0, UNITS, early)

    @pl.when(y_hi == 0)
    def _():
        arrived(2)
        share(2)
        arrived(6)
        share(6)
        arrived(8)
        share(8)

    @pl.when(y_hi == 1)
    def _():
        arrived(4)
        share(4)
        arrived(6)
        share(6)
        arrived(1)

    for slot in late[:3]:
        key_marks(slot)

    def arrive_last():
        @pl.when(y_hi == 0)
        def _():
            arrived(1)

            @pl.when(core == 0)
            def _():
                arrived(5)

            @pl.when(core == 1)
            def _():
                arrived(3)

        @pl.when(y_hi == 1)
        def _():
            arrived(3)
            arrived(5)

        arrived(7)
        for slot in late[3:]:
            key_marks(slot)

    w_copy.wait()

    def z_copy(kind, n):
        low, high = pl.ds(0, 64), pl.ds(64, 64)
        src, dst, peer = (
            (part_z.at[0, n, pl.ds(0, 32)], a_z.at[n, pl.ds(0, 32)], z_next),
            (part_z.at[0, n, pl.ds(64, 32)], b_z.at[n, pl.ds(0, 32)], z_prev),
            (part_z.at[1, n, high], up_z.at[n, high], z_next),
            (part_z.at[2, n, low], up_z.at[n, low], z_next),
            (part_z.at[1, n, low], down_z.at[n, low], z_prev),
            (part_z.at[2, n, high], down_z.at[n, high], z_prev),
            (mate_out.at[n], mate_in.at[n], y_mate),
            (part_z.at[0, n, pl.ds(32, 32)], a_z.at[n, pl.ds(32, 32)], z_next),
            (part_z.at[0, n, pl.ds(96, 32)], b_z.at[n, pl.ds(32, 32)], z_prev),
        )[kind]
        return pltpu.make_async_remote_copy(
            src_ref=src, dst_ref=dst, send_sem=z_send.at[kind, n], recv_sem=z_recv.at[kind, n],
            device_id=peer, device_id_type=MESH,
        )

    mine = pl.ds(pl.multiple_of(y_lo * 64, 64), 64)
    theirs = pl.ds(pl.multiple_of(64 - y_lo * 64, 64), 64)

    def way(t):
        return (t + y_lo) % 2

    def half_of(t, with_far):
        first = 32 * way(t) if with_far else 32 - 32 * way(t)
        return pl.ds(pl.multiple_of(first, 32), 32)

    def y_copy(kind, n):
        place = kind
        if kind == 0 or kind == 10:
            sub = kind // 10 * 32
            rows = pl.ds(pl.multiple_of(64 - y_lo * 64 + sub, 32), 32)
            src, dst, peer = part_y.at[0, n, rows], met_y.at[0, n, pl.ds(sub, 32)], y_mate
        elif kind < 4:
            src, dst, peer = part_y.at[kind, n, theirs], met_y.at[kind, n], y_mate
        elif kind < 6:
            src = sum_y.at[0, n, pl.ds(32 * (kind - 4), 32)]
            dst, peer = far_y.at[kind - 4, n], (z_next, z_prev)[kind - 4]
        else:
            t, with_far = kind // 2 - 2, kind % 2
            rows = half_of(t, with_far)
            src, dst, peer = sum_y.at[t, n, rows], near_y.at[way(t), n, rows], at_z(1 + 2 * way(t))
            place = 6 + 2 * way(t) + with_far
        return pltpu.make_async_remote_copy(
            src_ref=src, dst_ref=dst, send_sem=y_send.at[kind, n], recv_sem=y_recv.at[place, n],
            device_id=peer, device_id_type=MESH,
        )

    def meet(t):
        for n in range(NY):
            y_copy(t, n).wait_recv()
            if t == 0:
                y_copy(10, n).wait_recv()
            sum_y[t, n] = (part_y[t, n, mine].astype(f32) + met_y[t, n].astype(f32)).astype(bf16)
            for kind in ((4, 5), (6,), (8,))[t]:
                y_copy(kind, n).start()

    def add_far_z():
        for n in range(NZ):
            z_copy(0, n).wait_recv()
            z_copy(7, n).wait_recv()
            part_z[2, n, 0:64] = (part_z[2, n, 0:64].astype(f32) + a_z[n].astype(f32)).astype(bf16)
            z_copy(3, n).start()
            z_copy(1, n).wait_recv()
            z_copy(8, n).wait_recv()
            part_z[2, n, 64:128] = (part_z[2, n, 64:128].astype(f32) + b_z[n].astype(f32)).astype(bf16)
            z_copy(5, n).start()

    def add_far_y():
        for n in range(NY):
            y_copy(4, n).wait_recv()
            y_copy(5, n).wait_recv()
            for t in (1, 2):
                rows = half_of(t, 1)
                sum_y[t, n, rows] = (
                    sum_y[t, n, rows].astype(f32) + far_y[way(t), n].astype(f32)
                ).astype(bf16)
                y_copy(5 + 2 * t, n).start()

    for sub in range(2):
        if sub == 0:
            run(0, 2, late[:3])
            arrive_last()
            run(0, 2, late[3:])
        else:
            run(2, 2, late)
        for g in range(2):
            state = acc[2 * sub + g]
            rows = state[0:128] / state[128:129]
            for j in range(2):
                two_heads = rows[:, j * 128 : (j + 1) * 128].T.astype(bf16)
                for i in range(2):
                    head = 4 * g + 2 * j + i
                    att[0:64, head * 128 : (head + 1) * 128] = two_heads[i * 64 : (i + 1) * 64]

        for n in range(NY + NZ):
            piece = jnp.dot(
                att[0:64], w[:, n * PCOLS : (n + 1) * PCOLS], preferred_element_type=f32
            ).astype(bf16)
            into, i = (part_y, n) if n < NY else (part_z, n - NY)
            for half in range(2):
                place = half * 64 + sub * 32
                into[0, i, place : place + 32] = piece[half * 32 : (half + 1) * 32]
            if n == NY - 1:
                for i in range(NY):
                    y_copy((0, 10)[sub], i).start()
            if n == NY + 1 or n == NY + 3:
                for i in (n - NY - 1, n - NY):
                    for kind in ((0, 1), (7, 8))[sub]:
                        z_copy(kind, i).start()

    for t in range(1, 4):
        run(t * 4, 4, late)
        for g in range(4):
            state = acc[t * 4 + g]
            rows = state[0:128] / state[128:129]
            for j in range(2):
                head = 2 * g + j
                att[:, head * 128 : (head + 1) * 128] = rows[:, j * 128 : (j + 1) * 128].T.astype(bf16)

        for n in range(NY + NZ):
            piece = jnp.dot(
                att[...], w[:, n * PCOLS : (n + 1) * PCOLS], preferred_element_type=f32
            ).astype(bf16)
            if n < NY:
                part_y[t, n] = piece
            else:
                part_z[t, n - NY] = piece
            if n == NY - 1:
                for i in range(NY):
                    y_copy(t, i).start()
            if n == NY + 1 or n == NY + 3:
                for i in (n - NY - 1, n - NY):
                    for kind in ((), (2, 4), (), ())[t]:
                        z_copy(kind, i).start()
        meet(t - 1)
        if t == 2:
            add_far_z()

    add_far_y()

    def total_z(n, rows):
        return (
            part_z[3, n, rows].astype(f32) + up_z[n, rows].astype(f32) + down_z[n, rows].astype(f32)
        )

    for n in range(NZ):
        for kind in (2, 3, 4, 5):
            z_copy(kind, n).wait_recv()
        mate_out[n] = total_z(n, theirs).astype(bf16)
        z_copy(6, n).start()

    for n in range(NZ):
        one_ref[:, (NY + n) * PCOLS : (NY + n + 1) * PCOLS] = total_z(n, mine).astype(bf16)

    for n in range(NY):
        y_copy(3, n).wait_recv()
        one_ref[:, n * PCOLS : (n + 1) * PCOLS] = (
            part_y[3, n, mine].astype(f32) + met_y[3, n].astype(f32)
        ).astype(bf16)

    for n in range(NY):
        for kind in (6, 7, 8, 9):
            y_copy(kind, n).wait_recv()
        two_ref[:, n * PCOLS : (n + 1) * PCOLS] = (
            near_y[0, n].astype(f32) + near_y[1, n].astype(f32)
        ).astype(bf16)

    for n in range(NZ):
        z_copy(6, n).wait_recv()
        two_ref[:, (NY + n) * PCOLS : (NY + n + 1) * PCOLS] = mate_in[n]

    for send in (0, 1, 2, 3, 6, 7, 8, 9):
        kv_copy(0, 0, send, sibling).wait_send()

    @pl.when(y_hi == 0)
    def _():
        for send in (4, 5):
            kv_copy(0, 0, send, sibling).wait_send()

    for n in range(NZ):
        for kind in range(9):
            z_copy(kind, n).wait_send()
    for n in range(NY):
        for kind in range(11):
            y_copy(kind, n).wait_send()


def on_device(queries, key_states, value_states, doc_ids, out_weight):
    vmem = pl.BlockSpec(memory_space=pltpu.VMEM)
    in_hbm = [
        pltpu.with_memory_space_constraint(a, pltpu.HBM)
        for a in (queries, key_states, value_states, doc_ids.reshape(4, 128), out_weight)
    ]
    one, two = pl.pallas_call(
        kernel,
        name="attend_project",
        out_shape=[jax.ShapeDtypeStruct((64, D_OUT), bf16)] * 2,
        in_specs=[pl.BlockSpec(memory_space=pl.ANY)] * 5,
        out_specs=[vmem, vmem],
        scratch_shapes=[
            pltpu.VMEM((SLOTS + 2, BLOCK, 128), bf16),
            pltpu.VMEM((SLOTS, TOK, 128), bf16),
            pltpu.VMEM((UNITS, 256, 256), bf16),
            pltpu.VMEM((6 * TOK, 256), f32),
            pltpu.VMEM((6 * TOK, 256), f32),
            pltpu.VMEM((8, 256), f32),
            pltpu.VMEM((8, 256), f32),
            pltpu.VMEM((UNITS, 1, 256), f32),
            pltpu.VMEM((UNITS, VROWS, 256), f32),
            pltpu.VMEM((128, 1024), bf16),
            pltpu.VMEM((1024, D_OUT), bf16),
            pltpu.VMEM((4, NZ, 128, PCOLS), bf16),
            pltpu.VMEM((NZ, 64, PCOLS), bf16),
            pltpu.VMEM((NZ, 64, PCOLS), bf16),
            pltpu.VMEM((NZ, 128, PCOLS), bf16),
            pltpu.VMEM((NZ, 128, PCOLS), bf16),
            pltpu.VMEM((NZ, 64, PCOLS), bf16),
            pltpu.VMEM((NZ, 64, PCOLS), bf16),
            pltpu.VMEM((4, NY, 128, PCOLS), bf16),
            pltpu.VMEM((4, NY, 64, PCOLS), bf16),
            pltpu.VMEM((3, NY, 64, PCOLS), bf16),
            pltpu.VMEM((2, NY, 32, PCOLS), bf16),
            pltpu.VMEM((2, NY, 64, PCOLS), bf16),
            pltpu.SemaphoreType.DMA((10,)),
            pltpu.SemaphoreType.DMA((SLOTS + 2,)),
            pltpu.SemaphoreType.DMA((9, NZ)),
            pltpu.SemaphoreType.DMA((9, NZ)),
            pltpu.SemaphoreType.DMA((11, NY)),
            pltpu.SemaphoreType.DMA((11, NY)),
            pltpu.SemaphoreType.DMA,
            pltpu.VMEM((TOK, 1024), bf16),
            pltpu.VMEM((TOK, 128), bf16),
            pltpu.VMEM((4, 128), jnp.int32),
            pltpu.SemaphoreType.DMA((4,)),
        ],
        compiler_params=pltpu.CompilerParams(
            collective_id=0, has_side_effects=True, vmem_limit_bytes=52 * 2**20
        ),
        cost_estimate=pl.CostEstimate(
            flops=14 * 10**9, bytes_accessed=10 * 2**20, transcendentals=19 * 10**6
        ),
    )(*in_hbm)
    return (one.astype(f32) + two.astype(f32)).astype(bf16)


def solution(mesh):
    return jax.shard_map(
        on_device,
        mesh=mesh,
        in_specs=(P("ctx", "head"), P("ctx", "head"), P("ctx", "head"), P("ctx"), P("head", None)),
        out_specs=P(("ctx", "head"), None),
        check_vma=False,
    )
```

```python
import jax
import jax.numpy as jnp
from jax import lax
from jax.experimental import pallas as pl
from jax.experimental.pallas import tpu as pltpu
from jax.sharding import PartitionSpec as P

DH = 128
TOK = 512
VROWS = 144
IDS = 2 * TOK
BLOCK = IDS + 16
SLOTS = 9
RELAY_X, RELAY_Y = 9, 10
UNITS = 16
D_OUT = 4096
PCOLS = 1024
NY, NZ = 2, 2
EXP_SCALE = DH**-0.5 * 1.4426950408889634
FAR = -1e30
MESH = pl.DeviceIdType.MESH
NT = (((1,), (1,)), ((), ()))
bf16 = jnp.bfloat16
f32 = jnp.float32


def kernel(
    q_hbm, k_hbm, v_hbm, ids_hbm, w_hbm, one_ref, two_ref,
    kv, kf, qx, s0, s1, mx0, mx1, top, acc, att, w,
    part_z, a_z, b_z, up_z, down_z, mate_out, mate_in,
    part_y, met_y, sum_y, far_y, near_y,
    kv_send, kv_recv, z_send, z_recv, y_send, y_recv, w_sem, q_ref, v_ref, ids_ref, in_sem,
):
    c = lax.axis_index("ctx")
    h = lax.axis_index("head")
    x = c // 4
    y_hi = (c // 2) % 2
    core = c % 2
    y_lo = h // 4
    z = h % 4

    def at_x(step):
        return (((x + step) % 4) * 4 + y_hi * 2 + core, h)

    def at_z(step):
        return (c, y_lo * 4 + (z + step) % 4)

    x_next, x_prev, x_far = at_x(1), at_x(3), at_x(2)
    y_pair = (x * 4 + (1 - y_hi) * 2 + core, h)
    sibling = (x * 4 + y_hi * 2 + 1 - core, h)
    z_next, z_prev = at_z(1), at_z(3)
    y_mate = (c, (1 - y_lo) * 4 + z)

    ids_copy = pltpu.make_async_copy(ids_hbm, ids_ref, in_sem.at[0])
    ids_copy.start()
    v_copy = pltpu.make_async_copy(v_hbm, v_ref, in_sem.at[1])
    v_copy.start()
    k_copy = pltpu.make_async_copy(k_hbm, kv.at[0, pl.ds(0, TOK)], in_sem.at[2])
    k_copy.start()
    q_copy = pltpu.make_async_copy(q_hbm, q_ref, in_sem.at[3])
    q_copy.start()
    w_copy = pltpu.make_async_copy(w_hbm, w, w_sem)
    w_copy.start()

    barrier = pltpu.get_barrier_semaphore()
    for peer in (x_next, x_prev, x_far, y_pair, sibling, z_next, z_prev, y_mate):
        pl.semaphore_signal(barrier, inc=1, device_id=peer, device_id_type=MESH)

    ids_copy.wait()
    kv[0, IDS:BLOCK, :] = jnp.concatenate(
        [ids_ref[...].astype(f32), jnp.zeros((12, 128), f32)], axis=0
    ).astype(bf16)
    v_copy.wait()
    for r in range(4):
        kv[0, TOK + r * 128 : TOK + (r + 1) * 128, :] = (
            v_ref[r * 128 : (r + 1) * 128, :].astype(f32).T.astype(bf16)
        )
    k_copy.wait()

    pl.semaphore_wait(barrier, 8)

    def kv_copy(src, dst, send, peer):
        return pltpu.make_async_remote_copy(
            src_ref=kv.at[src],
            dst_ref=kv.at[dst],
            send_sem=kv_send.at[send],
            recv_sem=kv_recv.at[dst],
            device_id=peer,
            device_id_type=MESH,
        )

    def arrived(slot):
        kv_copy(slot, slot, 0, sibling).wait_recv()

    @pl.when(y_hi == 0)
    def _():
        kv_copy(0, 4, 0, x_next).start()
        kv_copy(0, 2, 1, y_pair).start()
        kv_copy(0, RELAY_X, 2, x_prev).start()

    @pl.when(y_hi == 1)
    def _():
        kv_copy(0, 8, 0, x_far).start()
        kv_copy(0, RELAY_Y, 1, y_pair).start()

    def share(slot):
        @pl.when(core == 0)
        def _():
            if slot < 8:
                kv_copy(slot, slot + 1, 6 + slot // 2, sibling).start()

        @pl.when(core == 1)
        def _():
            if slot > 0:
                kv_copy(slot, slot - 1, 5 + slot // 2, sibling).start()

    share(0)

    lane = lax.broadcasted_iota(jnp.int32, (128, 128), 1).astype(f32)

    def id_columns(slot, r):
        row = kv[slot, IDS:BLOCK, :].astype(f32)[r : r + 1, :]
        return jnp.broadcast_to(row, (128, 128)).T

    def key_marks(slot):
        shift = jnp.where(c >= slot, 0.0, 1000.0)
        for r in range(4):
            kf[slot, r * 128 : (r + 1) * 128, :] = jnp.where(
                id_columns(slot, r) + shift == lane, 0.0, FAR
            ).astype(bf16)

    order = ((2, 2), (3, 1), (1, 3), (0, 0))
    firsts = [(((z + low) % 4) * 64, ((z + high) % 4) * 64 + 256) for low, high in order]

    q_copy.wait()

    for r in range(4):
        kf[0, r * 128 : (r + 1) * 128, :] = jnp.where(id_columns(0, r) == lane, 1.0, 0.0).astype(bf16)
    for t in range(4):
        for half in range(2):
            rows = pl.ds(pl.multiple_of(firsts[t][half], 64), 64)
            marks = kf[0, rows, :]
            for g in range(4):
                for j in range(2):
                    place = j * 128 + half * 64
                    head = 2 * g + j
                    qx[t * 4 + g, place : place + 64, 0:128] = q_ref[rows, head * 128 : (head + 1) * 128]
                    qx[t * 4 + g, place : place + 64, 128:256] = marks
    key_marks(0)

    ones = jnp.ones((VROWS - 128, TOK), bf16)
    key_index = lax.broadcasted_iota(jnp.int32, (TOK, 256), 0)
    lane_q = lax.broadcasted_iota(jnp.int32, (1, 256), 1) % 128

    def score(unit, slot, i, s_ref, diagonal):
        keys = jnp.concatenate([kv[slot, 0:TOK, :], kf[slot]], axis=1)
        s = lax.dot_general(keys, qx[unit], NT, preferred_element_type=f32)
        if diagonal:
            t = unit // 4
            low = jnp.where(t == 0, 2, jnp.where(t == 1, 3, jnp.where(t == 2, 1, 0)))
            high = jnp.where(t == 0, 2, jnp.where(t == 1, 1, jnp.where(t == 2, 3, 0)))
            low_first = ((z + low) % 4) * 64
            high_first = ((z + high) % 4) * 64 + 192
            q_index = lane_q + jnp.where(lane_q < 64, low_first, high_first)
            s = jnp.where(key_index <= q_index, s, FAR)
        s_ref[i * TOK : (i + 1) * TOK, :] = s
        return jnp.max(s.reshape(TOK // 8, 8, 256), axis=0)

    def weigh(slot, i, s_ref, new_top):
        values = jnp.concatenate(
            [kv[slot, TOK + r * 128 : TOK + (r + 1) * 128, :] for r in range(4)], axis=1
        )
        values = jnp.concatenate([values, ones], axis=0)
        probs = jnp.exp2((s_ref[i * TOK : (i + 1) * TOK, :] - new_top) * EXP_SCALE).astype(bf16)
        return jnp.dot(values, probs, preferred_element_type=f32)

    def stage(ahead, now, slots, into, held, diagonal):
        if now is not None:
            new_top = jnp.max(held[1][...], axis=0, keepdims=True)
            if not diagonal:
                old_top = top[now]
                new_top = jnp.maximum(old_top, new_top)
        highest, add = None, None
        for i, slot in enumerate(slots):
            if ahead is not None:
                here = score(ahead, slot, i, into[0], diagonal)
                highest = here if highest is None else jnp.maximum(highest, here)
            if now is not None:
                here = weigh(slot, i, held[0], new_top)
                add = here if add is None else add + here
        if ahead is not None:
            into[1][...] = highest
        if now is not None:
            if diagonal:
                acc[now] = add
            else:
                acc[now] = acc[now] * jnp.exp2((old_top - new_top) * EXP_SCALE) + add
            top[now] = new_top

    pair = ((s0, mx0), (s1, mx1))

    def run(first, count, slots, diagonal=False):
        stage(first, None, slots, pair[0], None, diagonal)

        def body(i, carry):
            for e in range(4):
                now = first + 4 * i + e
                ahead = now + 1
                if e == 3:
                    ahead = None if count == 4 else jnp.minimum(ahead, first + count - 1)
                stage(ahead, now, slots, pair[(e + 1) % 2], pair[e % 2], diagonal)
            return carry

        if count == 4:
            body(0, 0)
        else:
            lax.fori_loop(0, count // 4, body, 0)

    run(0, UNITS, (0,), True)

    @pl.when(y_hi == 0)
    def _():
        arrived(4)
        kv_copy(4, 6, 3, y_pair).start()
        share(4)
        arrived(RELAY_X)
        kv_copy(RELAY_X, 8, 4, x_prev).start()
        arrived(RELAY_Y)
        kv_copy(RELAY_Y, 2, 5, x_next).start()

    @pl.when(y_hi == 1)
    def _():
        arrived(8)
        kv_copy(8, 6, 3, y_pair).start()
        kv_copy(0, 4, 2, x_next).start()
        share(8)
        arrived(2)
        share(2)

    early = (4 + 4 * y_hi, 2 * y_hi + (1 - y_hi) * (3 + 2 * core))
    late = (
        2 - y_hi, 6 - 2 * y_hi, 8 - 2 * y_hi, 1 + 2 * y_hi, 5 - 2 * core * (1 - y_hi), 7,
    )
    key_marks(early[0])

    @pl.when(y_hi == 0)
    def _():
        @pl.when(core == 0)
        def _():
            arrived(3)

        @pl.when(core == 1)
        def _():
            arrived(5)

    key_marks(early[1])
    run(0, UNITS, early)

    @pl.when(y_hi == 0)
    def _():
        arrived(2)
        share(2)
        arrived(6)
        share(6)
        arrived(8)
        share(8)

    @pl.when(y_hi == 1)
    def _():
        arrived(4)
        share(4)
        arrived(6)
        share(6)
        arrived(1)

    for slot in late[:3]:
        key_marks(slot)

    def arrive_last():
        @pl.when(y_hi == 0)
        def _():
            arrived(1)

            @pl.when(core == 0)
            def _():
                arrived(5)

            @pl.when(core == 1)
            def _():
                arrived(3)

        @pl.when(y_hi == 1)
        def _():
            arrived(3)
            arrived(5)

        arrived(7)
        for slot in late[3:]:
            key_marks(slot)

    w_copy.wait()

    def z_copy(kind, n):
        low, high = pl.ds(0, 64), pl.ds(64, 64)
        src, dst, peer = (
            (part_z.at[0, n, low], a_z.at[n], z_next),
            (part_z.at[0, n, high], b_z.at[n], z_prev),
            (part_z.at[1, n, high], up_z.at[n, high], z_next),
            (part_z.at[2, n, low], up_z.at[n, low], z_next),
            (part_z.at[1, n, low], down_z.at[n, low], z_prev),
            (part_z.at[2, n, high], down_z.at[n, high], z_prev),
            (mate_out.at[n], mate_in.at[n], y_mate),
        )[kind]
        return pltpu.make_async_remote_copy(
            src_ref=src, dst_ref=dst, send_sem=z_send.at[kind, n], recv_sem=z_recv.at[kind, n],
            device_id=peer, device_id_type=MESH,
        )

    mine = pl.ds(pl.multiple_of(y_lo * 64, 64), 64)
    theirs = pl.ds(pl.multiple_of(64 - y_lo * 64, 64), 64)

    def way(t):
        return (t + y_lo) % 2

    def half_of(t, with_far):
        first = 32 * way(t) if with_far else 32 - 32 * way(t)
        return pl.ds(pl.multiple_of(first, 32), 32)

    def y_copy(kind, n):
        place = kind
        if kind < 4:
            src, dst, peer = part_y.at[kind, n, theirs], met_y.at[kind, n], y_mate
        elif kind < 6:
            src = sum_y.at[0, n, pl.ds(32 * (kind - 4), 32)]
            dst, peer = far_y.at[kind - 4, n], (z_next, z_prev)[kind - 4]
        else:
            t, with_far = kind // 2 - 2, kind % 2
            rows = half_of(t, with_far)
            src, dst, peer = sum_y.at[t, n, rows], near_y.at[way(t), n, rows], at_z(1 + 2 * way(t))
            place = 6 + 2 * way(t) + with_far
        return pltpu.make_async_remote_copy(
            src_ref=src, dst_ref=dst, send_sem=y_send.at[kind, n], recv_sem=y_recv.at[place, n],
            device_id=peer, device_id_type=MESH,
        )

    def meet(t):
        for n in range(NY):
            y_copy(t, n).wait_recv()
            sum_y[t, n] = (part_y[t, n, mine].astype(f32) + met_y[t, n].astype(f32)).astype(bf16)
            for kind in ((4, 5), (6,), (8,))[t]:
                y_copy(kind, n).start()

    def add_far_z():
        for n in range(NZ):
            z_copy(0, n).wait_recv()
            part_z[2, n, 0:64] = (part_z[2, n, 0:64].astype(f32) + a_z[n].astype(f32)).astype(bf16)
            z_copy(3, n).start()
            z_copy(1, n).wait_recv()
            part_z[2, n, 64:128] = (part_z[2, n, 64:128].astype(f32) + b_z[n].astype(f32)).astype(bf16)
            z_copy(5, n).start()

    def add_far_y():
        for n in range(NY):
            y_copy(4, n).wait_recv()
            y_copy(5, n).wait_recv()
            for t in (1, 2):
                rows = half_of(t, 1)
                sum_y[t, n, rows] = (
                    sum_y[t, n, rows].astype(f32) + far_y[way(t), n].astype(f32)
                ).astype(bf16)
                y_copy(5 + 2 * t, n).start()

    for t in range(4):
        if t == 0:
            run(0, 4, late[:3])
            arrive_last()
            run(0, 4, late[3:])
        else:
            run(t * 4, 4, late)
        for g in range(4):
            state = acc[t * 4 + g]
            rows = state[0:128] / state[128:129]
            for j in range(2):
                head = 2 * g + j
                att[:, head * 128 : (head + 1) * 128] = rows[:, j * 128 : (j + 1) * 128].T.astype(bf16)

        for n in range(NY + NZ):
            piece = jnp.dot(
                att[...], w[:, n * PCOLS : (n + 1) * PCOLS], preferred_element_type=f32
            ).astype(bf16)
            if n < NY:
                part_y[t, n] = piece
            else:
                part_z[t, n - NY] = piece
            if n == NY - 1:
                for i in range(NY):
                    y_copy(t, i).start()
            if n == NY + 1:
                for i in (n - NY - 1, n - NY):
                    for kind in ((0, 1), (2, 4), (), ())[t]:
                        z_copy(kind, i).start()
        if t > 0:
            meet(t - 1)
        if t == 2:
            add_far_z()

    add_far_y()

    def total_z(n, rows):
        return (
            part_z[3, n, rows].astype(f32) + up_z[n, rows].astype(f32) + down_z[n, rows].astype(f32)
        )

    for n in range(NZ):
        for kind in (2, 3, 4, 5):
            z_copy(kind, n).wait_recv()
        mate_out[n] = total_z(n, theirs).astype(bf16)
        z_copy(6, n).start()

    for n in range(NZ):
        one_ref[:, (NY + n) * PCOLS : (NY + n + 1) * PCOLS] = total_z(n, mine).astype(bf16)

    for n in range(NY):
        y_copy(3, n).wait_recv()
        one_ref[:, n * PCOLS : (n + 1) * PCOLS] = (
            part_y[3, n, mine].astype(f32) + met_y[3, n].astype(f32)
        ).astype(bf16)

    for n in range(NY):
        for kind in (6, 7, 8, 9):
            y_copy(kind, n).wait_recv()
        two_ref[:, n * PCOLS : (n + 1) * PCOLS] = (
            near_y[0, n].astype(f32) + near_y[1, n].astype(f32)
        ).astype(bf16)

    for n in range(NZ):
        z_copy(6, n).wait_recv()
        two_ref[:, (NY + n) * PCOLS : (NY + n + 1) * PCOLS] = mate_in[n]

    for send in (0, 1, 2, 3, 6, 7, 8, 9):
        kv_copy(0, 0, send, sibling).wait_send()

    @pl.when(y_hi == 0)
    def _():
        for send in (4, 5):
            kv_copy(0, 0, send, sibling).wait_send()

    for n in range(NZ):
        for kind in range(7):
            z_copy(kind, n).wait_send()
    for n in range(NY):
        for kind in range(10):
            y_copy(kind, n).wait_send()


def on_device(queries, key_states, value_states, doc_ids, out_weight):
    vmem = pl.BlockSpec(memory_space=pltpu.VMEM)
    in_hbm = [
        pltpu.with_memory_space_constraint(a, pltpu.HBM)
        for a in (queries, key_states, value_states, doc_ids.reshape(4, 128), out_weight)
    ]
    one, two = pl.pallas_call(
        kernel,
        name="attend_project",
        out_shape=[jax.ShapeDtypeStruct((64, D_OUT), bf16)] * 2,
        in_specs=[pl.BlockSpec(memory_space=pl.ANY)] * 5,
        out_specs=[vmem, vmem],
        scratch_shapes=[
            pltpu.VMEM((SLOTS + 2, BLOCK, 128), bf16),
            pltpu.VMEM((SLOTS, TOK, 128), bf16),
            pltpu.VMEM((UNITS, 256, 256), bf16),
            pltpu.VMEM((6 * TOK, 256), f32),
            pltpu.VMEM((6 * TOK, 256), f32),
            pltpu.VMEM((8, 256), f32),
            pltpu.VMEM((8, 256), f32),
            pltpu.VMEM((UNITS, 1, 256), f32),
            pltpu.VMEM((UNITS, VROWS, 256), f32),
            pltpu.VMEM((128, 1024), bf16),
            pltpu.VMEM((1024, D_OUT), bf16),
            pltpu.VMEM((4, NZ, 128, PCOLS), bf16),
            pltpu.VMEM((NZ, 64, PCOLS), bf16),
            pltpu.VMEM((NZ, 64, PCOLS), bf16),
            pltpu.VMEM((NZ, 128, PCOLS), bf16),
            pltpu.VMEM((NZ, 128, PCOLS), bf16),
            pltpu.VMEM((NZ, 64, PCOLS), bf16),
            pltpu.VMEM((NZ, 64, PCOLS), bf16),
            pltpu.VMEM((4, NY, 128, PCOLS), bf16),
            pltpu.VMEM((4, NY, 64, PCOLS), bf16),
            pltpu.VMEM((3, NY, 64, PCOLS), bf16),
            pltpu.VMEM((2, NY, 32, PCOLS), bf16),
            pltpu.VMEM((2, NY, 64, PCOLS), bf16),
            pltpu.SemaphoreType.DMA((10,)),
            pltpu.SemaphoreType.DMA((SLOTS + 2,)),
            pltpu.SemaphoreType.DMA((7, NZ)),
            pltpu.SemaphoreType.DMA((7, NZ)),
            pltpu.SemaphoreType.DMA((10, NY)),
            pltpu.SemaphoreType.DMA((10, NY)),
            pltpu.SemaphoreType.DMA,
            pltpu.VMEM((TOK, 1024), bf16),
            pltpu.VMEM((TOK, 128), bf16),
            pltpu.VMEM((4, 128), jnp.int32),
            pltpu.SemaphoreType.DMA((4,)),
        ],
        compiler_params=pltpu.CompilerParams(
            collective_id=0, has_side_effects=True, vmem_limit_bytes=52 * 2**20
        ),
        cost_estimate=pl.CostEstimate(
            flops=14 * 10**9, bytes_accessed=10 * 2**20, transcendentals=19 * 10**6
        ),
    )(*in_hbm)
    return (one.astype(f32) + two.astype(f32)).astype(bf16)


def solution(mesh):
    return jax.shard_map(
        on_device,
        mesh=mesh,
        in_specs=(P("ctx", "head"), P("ctx", "head"), P("ctx", "head"), P("ctx"), P("head", None)),
        out_specs=P(("ctx", "head"), None),
        check_vma=False,
    )
```
